512 devices in a mesh: pool: 8 (over y), seq: 16 (over z, core), head: 4 (over x).
Axes of the slice: x: 4, y: 8, z: 8, core: 2. Of those that a mesh axis runs over, the one named last changes fastest.
Arguments:
- latents: bfloat16 [16384, 2048], P(('pool', 'seq'), 'head'), may hold values from -6 to 6
- route: int32 [16384], P(('pool', 'seq')), may hold values from 0 to 16383, as said below
- seg_lengths: int32 [8, 8], P('pool'), may hold values from 1 to 1024, 2048 in all within a row
- modulation: float32 [8, 8, 6144], P('pool'), may hold values from -3 to 3
- qkv_weight: bfloat16 [2048, 3, 1024], P(None, None, 'head'), may hold values from -0.125 to 0.125
- qk_gain: float32 [2, 64], replicated, may hold values from 0.5 to 16
- out_weight: bfloat16 [1024, 2048], P('head'), may hold values from -0.1875 to 0.1875
Outputs:
- blended: bfloat16 [16384, 2048], P(('pool', 'seq'), 'head')
The draws below stay inside these ranges and needn't reach their ends.
Inputs may be any that keep to these rules, and one draw needn't show every extreme that they name: route is a permutation of the packed positions; position p lies on device p // 128 of pool+seq (pool slowest) at row p % 128. Of the 128 rows of one device at most 2 have positions on any one device, and some device sends exactly 2 to some device.
All inputs are finite; a program needn't handle non-finite values.
Results may differ from the reference program's by a relative error of at most 0.014.
The reference program's roundings to bfloat16 on the way (of `packed`, `normed`, `attended` and `mixed`) count: a program that leaves them out, or rounds other values in their place, can miss the bound.
Values may be sent and summed in bfloat16 or wider, within the bound.
A program may use at most 64 MiB of HBM per device.

```python
import math
import jax
import jax.numpy as jnp
import numpy as np
from jax import lax

D = 2048
HEADS = 16
HEAD_DIM = 64
TOK_DEV = 128
SEGS = 8
GROUP = 2048
ROWS = 16384
CAP = 2
SEG_MOST = 1024
N_POOL = 8


def draw_route(key, part):
    key = jax.random.fold_in(key, 3)
    peers = ROWS // TOK_DEV
    base = CAP // 2
    quarter = peers // 4
    others = jnp.concatenate([jnp.full((quarter - 1,), base, jnp.int32), jnp.full((quarter,), -base, jnp.int32), jnp.zeros((peers - 2 * quarter,), jnp.int32)])
    others = jax.random.permutation(jax.random.fold_in(key, 1), others)
    moves = jnp.concatenate([others[:peers // 2], jnp.full((1,), base, jnp.int32), others[peers // 2:]])
    source = jnp.arange(peers).astype(jnp.int32)
    counts = base + moves[(source[None, :] - source[:, None]) % peers]
    inclusive = jnp.cumsum(counts, axis=1)
    exclusive = inclusive - counts
    before = jnp.cumsum(counts, axis=0) - counts
    within = jnp.arange(TOK_DEV).astype(jnp.int32)
    target = jnp.sum((within[None, :, None] >= inclusive[:, None, :]).astype(jnp.int32), axis=2)
    rank = within[None, :] - jnp.take_along_axis(exclusive, target, axis=1)
    arrival = jnp.take_along_axis(before, target, axis=1) + rank
    slot_keys = jax.random.split(jax.random.fold_in(key, 2), peers)
    slot_perm = jax.vmap(lambda k: jax.random.permutation(k, TOK_DEV))(slot_keys).astype(jnp.int32)
    slot = slot_perm[target, arrival]
    position = target * TOK_DEV + slot
    row_keys = jax.random.split(jax.random.fold_in(key, 4), peers)
    row_perm = jax.vmap(lambda k: jax.random.permutation(k, TOK_DEV))(row_keys).astype(jnp.int32)
    owner_row = (source[:, None] * TOK_DEV + row_perm).reshape(-1)
    return jnp.zeros((ROWS,), jnp.int32).at[owner_row].set(position.reshape(-1).astype(jnp.int32))


def draw_qk_gain(key, part):
    key = jax.random.fold_in(key, 7)
    gains = jnp.exp(jax.random.uniform(key, (2, HEAD_DIM), jnp.float32, jnp.log(0.5), jnp.log(2.0)))
    return gains


def levels(rng, shape, shards, smallest, high):
    def one(dim, parts):
        heights = jax.random.uniform(jax.random.fold_in(jax.random.fold_in(rng, 6), dim), (parts,), jnp.float32, smallest / len(shards), high / len(shards))
        return jnp.repeat(jnp.exp(heights), shape[dim] // parts).reshape((-1,) + (1,) * (len(shape) - dim - 1))

    level = one(*shards[0])
    for cut in shards[1:]:
        level = level * one(*cut)
    return level


def profile(amount, total, most, slope):
    portions = [(1 << 20) // math.isqrt(standing ** slope) + 1 for standing in range(2, amount + 1)]
    spare, given = total - most - (amount - 1), [1] * (amount - 1)
    while spare > 0:
        movable = [i for i in range(amount - 1) if given[i] < most]
        mass, remaining = sum([portions[i] for i in movable]), spare
        for i in movable:
            more = min(most - given[i], max(1, remaining * portions[i] // mass), spare)
            given[i] = given[i] + more
            spare = spare - more
    return np.array([most] + given)


def uneven_parts(key, number_of, total, limit, slope):
    if number_of == 2:
        one = jax.random.randint(key, (), max(1, total - limit), min(limit, total - 1) + 1)
        return jnp.stack([one, total - one])
    tallies = jnp.asarray(profile(number_of, total, limit, slope), jnp.int32)
    pairs = (number_of - 1) // 2
    donor, taker = tallies[1:1 + 2 * pairs:2], tallies[2:2 + 2 * pairs:2]
    room = jnp.minimum(donor - 1, limit - taker)
    moved = jax.random.randint(jax.random.fold_in(key, 1), (pairs,), 0, 1 << 20) % (room + 1)
    tallies = tallies.at[1:1 + 2 * pairs:2].set(donor - moved).at[2:2 + 2 * pairs:2].set(taker + moved)
    return tallies[jax.random.permutation(jax.random.fold_in(key, 2), number_of)]


def scatter_about(own_key, extent, deviation, bound, cuts=(), dtype=jnp.bfloat16):
    level = levels(own_key, extent, cuts, -0.22, 0.18) if cuts else 1.0
    drawn = jax.random.normal(own_key, extent, jnp.float32) * deviation * level
    return jnp.minimum(jnp.maximum(drawn, -bound), bound).astype(dtype)


def setup_inputs(seed: int = 0) -> dict:
    key_of = jax.random.split(jax.random.key(seed), 8)
    latents = scatter_about(key_of[0], (ROWS, D), 1.0, 6.0, ((0, 128), (1, 4)))
    route = draw_route(jax.random.fold_in(key_of[7], 71), 0)
    seg_lengths = jax.vmap(lambda own: uneven_parts(own, SEGS, GROUP, SEG_MOST, 2))(jax.random.split(key_of[2], N_POOL)).reshape((N_POOL, SEGS)).astype(jnp.int32)
    modulation = scatter_about(key_of[3], (N_POOL, SEGS, 3 * D), 0.5, 3.0, ((0, 8),), jnp.float32)
    qkv_weight = scatter_about(key_of[4], (D, 3, HEADS * HEAD_DIM), D ** -0.5, 0.125, ((2, 4),))
    qk_gain = draw_qk_gain(jax.random.fold_in(key_of[7], 71), 0)
    out_weight = scatter_about(key_of[6], (HEADS * HEAD_DIM, D), (HEADS * HEAD_DIM) ** -0.5, 0.1875, ((0, 4),))
    return {"latents": latents, "route": route, "seg_lengths": seg_lengths, "modulation": modulation, "qkv_weight": qkv_weight, "qk_gain": qk_gain, "out_weight": out_weight}


eps_norm = 1e-06
masked_score = -1e+30

def rms_scaled(values, gain):
    mean_sq = lax.optimization_barrier(jnp.mean(values * values, axis=-1, keepdims=True))
    return (values * lax.rsqrt(mean_sq + eps_norm) * gain).astype(jnp.bfloat16)

def one_group(group_rows, lengths, table, qkv_weight, qk_gain, out_weight):
    ends = jnp.cumsum(lengths)
    where_at = jnp.arange(GROUP).astype(jnp.int32)
    seg = lax.optimization_barrier(jnp.sum((where_at[:, None] >= ends[None, :]).astype(jnp.int32), axis=1))
    pick = (seg[:, None] == jnp.arange(SEGS).astype(jnp.int32)[None, :]).astype(jnp.float32)
    factors = jnp.dot(pick, table, precision=lax.Precision.HIGHEST)
    shift = factors[:, :D]
    scale = factors[:, D:2 * D]
    gate = factors[:, 2 * D:]
    feats = group_rows.astype(jnp.float32)
    centred = feats - lax.optimization_barrier(jnp.mean(feats, axis=1, keepdims=True))
    var = lax.optimization_barrier(jnp.mean(centred * centred, axis=1, keepdims=True))
    normed = (centred * lax.rsqrt(var + eps_norm) * (1.0 + scale) + shift).astype(jnp.bfloat16)
    query = jnp.dot(normed, qkv_weight[:, 0], preferred_element_type=jnp.float32)
    keys = jnp.dot(normed, qkv_weight[:, 1], preferred_element_type=jnp.float32)
    values = jnp.dot(normed, qkv_weight[:, 2], preferred_element_type=jnp.float32)
    query = rms_scaled(query.reshape(GROUP, HEADS, HEAD_DIM), qk_gain[0]).transpose(1, 0, 2)
    keys = rms_scaled(keys.reshape(GROUP, HEADS, HEAD_DIM), qk_gain[1]).transpose(1, 0, 2)
    values = values.reshape(GROUP, HEADS, HEAD_DIM).astype(jnp.bfloat16).transpose(1, 0, 2)
    qblock = math.gcd(GROUP, 512)
    score_scale = 1.0 / math.sqrt(HEAD_DIM)

    def attend_head(operands):
        head_q, head_k, head_v = operands

        def block(start):
            block_q = lax.dynamic_slice_in_dim(head_q, start, qblock, 0)
            block_seg = lax.dynamic_slice_in_dim(seg, start, qblock, 0)
            scores = jnp.dot(block_q, head_k.T, preferred_element_type=jnp.float32) * score_scale
            same = block_seg[:, None] == seg[None, :]
            scores = jnp.where(same, scores, masked_score)
            top = lax.optimization_barrier(jnp.max(scores, axis=1, keepdims=True))
            weights = jnp.where(same, jnp.exp(scores - top), 0.0)
            total = lax.optimization_barrier(jnp.sum(weights, axis=1, keepdims=True))
            summed = jnp.dot(weights.astype(jnp.bfloat16), head_v, preferred_element_type=jnp.float32)
            return (summed / total).astype(jnp.bfloat16)
        starts = (jnp.arange(GROUP // qblock) * qblock).astype(jnp.int32)
        return lax.map(block, starts).reshape(GROUP, HEAD_DIM)
    attended = lax.map(attend_head, (query, keys, values))
    attended = attended.transpose(1, 0, 2).reshape(GROUP, HEADS * HEAD_DIM)
    projected = jnp.dot(attended, out_weight, preferred_element_type=jnp.float32)
    return (feats + gate * projected).astype(jnp.bfloat16)

def reference(latents, route, seg_lengths, modulation, qkv_weight, qk_gain, out_weight):
    packed = jnp.zeros_like(latents).at[route].set(latents)
    groups = packed.reshape(ROWS // GROUP, GROUP, D)

    def run(operands):
        group_rows, lengths, table = operands
        return one_group(group_rows, lengths, table, qkv_weight, qk_gain, out_weight)
    mixed = lax.map(run, (groups, seg_lengths, modulation)).reshape(ROWS, D)
    return mixed[route]
```

```python
import functools

import jax
import jax.numpy as jnp
from jax import lax
from jax.experimental import pallas as pl
from jax.experimental.pallas import tpu as pltpu
from jax.sharding import PartitionSpec as P

MESH = pl.DeviceIdType.MESH
HEAD_DIM = 64
EPS = 1e-06
MASKED = -1e30
BF = jnp.bfloat16
F32 = jnp.float32
I32 = jnp.int32


def mm(a, b):
    return lax.dot_general(a, b, (((1,), (0,)), ((), ())), preferred_element_type=F32)


def nt(a, b):
    return lax.dot_general(a, b, (((1,), (1,)), ((), ())), preferred_element_type=F32)


def iota(shape, dim):
    return lax.broadcasted_iota(I32, shape, dim)


def onehot(cond):
    return jnp.where(cond, 1.0, 0.0).astype(BF)


def split3(x):
    hi = x.astype(BF).astype(F32)
    mid = (x - hi).astype(BF).astype(F32)
    return hi, mid, x - hi - mid


def signal(sem, **ids):
    pl.semaphore_signal(sem, inc=1, device_id=ids, device_id_type=MESH)


def remote(src, dst, send, recv, **ids):
    return pltpu.make_async_remote_copy(
        src_ref=src, dst_ref=dst, send_sem=send, recv_sem=recv, device_id=ids, device_id_type=MESH
    )


def drain(ref, sem):
    pltpu.make_async_copy(ref, ref, sem).wait()


def kernel(
    np_, ns, nh,
    lat_ref, route_ref, len_ref, gain_ref, mod_hbm, w_hbm, wo_hbm,
    out_ref,
    sb, rb, sb2, rb2, rtab, xbuf, og, modv, wv, wov, wo_all, gsrc, gbuf,
    kbuf, vbuf, scale_ref, shift_ref, acc_ref,
    stage_sem, load_sem,
    rz_s, rz_r, ry_s, ry_r, d_s, d_r, wo_s, wo_r, wc_s, wc_r, x_s, x_r, g_s, g_r,
    k_s, k_r, c_s, c_r, b_s, b_r, o_s, o_r,
):
    p, s, h = lax.axis_index("pool"), lax.axis_index("seq"), lax.axis_index("head")
    z, core = s // 2, lax.rem(s, 2)
    sib = s + 1 - 2 * core
    nz = ns // 2
    peers = np_ * ns
    me = p * ns + s
    rows, cols = lat_ref.shape
    width = cols * nh

    barrier = pltpu.get_barrier_semaphore()
    for k in range(1, ns):
        signal(barrier, seq=lax.rem(s + k, ns))
    for k in range(1, np_):
        signal(barrier, pool=lax.rem(p + k, np_))
    for k in range(1, nh):
        signal(barrier, head=lax.rem(h + k, nh))

    loads = [
        pltpu.make_async_copy(mod_hbm, modv, load_sem.at[0]),
        pltpu.make_async_copy(w_hbm, wv, load_sem.at[1]),
        pltpu.make_async_copy(wo_hbm, wov, load_sem.at[2]),
    ]
    for c in loads:
        c.start()

    rt = route_ref[...]
    r_row = jnp.broadcast_to(rt, (rows, rows))
    r_col = jnp.transpose(r_row.astype(F32)).astype(I32)
    t_row, t_col = r_row >> 7, r_col >> 7
    i0, i1 = iota((rows, rows), 0), iota((rows, rows), 1)
    same_t = t_row == t_col
    rank_row = jnp.sum(jnp.where(same_t & (i0 < i1), 1.0, 0.0), axis=0, keepdims=True).astype(I32)
    rank_col = jnp.sum(jnp.where(same_t & (i1 < i0), 1.0, 0.0), axis=1, keepdims=True).astype(I32)
    lat = lat_ref[...]
    blocks = cols // 128
    code = (rt >> 7) * (2 * blocks) + rank_row * blocks
    big = iota((peers * 2 * blocks, rows), 0)
    spread = jnp.concatenate([onehot(big == code + cb) for cb in range(blocks)], axis=1)
    stacked = jnp.concatenate([lat[:, cb * 128 : (cb + 1) * 128] for cb in range(blocks)], axis=0)
    sb[...] = mm(spread, stacked).reshape(peers, 2 * blocks, 128).astype(BF)
    rtab[me, 0] = rt[0]

    pl.semaphore_wait(barrier, ns + np_ + nh - 3)
    for k in range(1, np_):
        signal(stage_sem, pool=lax.rem(p + k, np_))
    pl.semaphore_wait(stage_sem, np_ - 1)

    for k in range(1, ns):
        remote(rtab.at[me], rtab.at[me], rz_s, rz_r, seq=lax.rem(s + k, ns)).start()

    def send_rows(k, carry):
        t = lax.rem(me + k, peers)
        remote(sb.at[t], rb.at[me], d_s, d_r, pool=t // ns, seq=lax.rem(t, ns)).start()
        return carry

    lax.fori_loop(1, peers, send_rows, 0)
    rb[me] = sb[me]

    loads[2].wait()
    half = wov.shape[0] // 2
    mine = pl.ds(pl.multiple_of(core * half, half), half)
    other = pl.ds(pl.multiple_of((1 - core) * half, half), half)
    wo_sends = []
    for k in range(1, nh):
        t = lax.rem(h + k, nh)
        cp = remote(
            wov.at[mine, pl.ds(pl.multiple_of(t * cols, cols), cols)], wo_all.at[h, mine],
            wo_s.at[k], wo_r.at[k], head=t,
        )
        cp.start()
        wo_sends.append(cp)
    wo_all[h] = wov[:, pl.ds(pl.multiple_of(h * cols, cols), cols)]

    drain(rtab.at[pl.ds(0, ns - 1)], rz_r)
    own_line = rtab.at[pl.ds(pl.multiple_of(p * ns, ns), ns)]
    for k in range(1, np_):
        remote(own_line, own_line, ry_s, ry_r, pool=lax.rem(p + k, np_)).start()

    ends = []
    total = 0
    for k in range(8):
        total = total + len_ref[0, k]
        ends.append(total)
    starts = [0] + ends[:7]

    def lane_row(n, values, offset, period):
        lane = iota((1, n), 1)
        out = jnp.zeros((1, n), I32)
        for k in range(8):
            hit = (lane & (period - 1)) == offset + k
            out = jnp.where(hit, values[k], out)
        return out

    pos32 = s * rows + iota((rows, 32), 0)
    pick = onehot(
        (pos32 >= lane_row(32, starts, 0, 8)) & (pos32 < lane_row(32, ends, 0, 8)) & (iota((rows, 32), 1) < 24)
    )
    loads[0].wait()
    step = 1024
    for c in range(0, 2 * width, step):
        hi, mid, lo = split3(modv[:, c : c + step])
        table = jnp.concatenate([hi, mid, lo, jnp.zeros_like(lo)], axis=0).astype(BF)
        part = mm(pick, table)
        if c < width:
            shift_ref[:, c : c + step] = part
        else:
            scale_ref[:, c - width : c - width + step] = 1.0 + part
    gsrc[:, :cols] = modv[:, pl.ds(pl.multiple_of(2 * width + h * cols, cols), cols)]
    lane = iota((1, 128), 1)
    end_l, start_l = jnp.zeros((1, 128), I32), jnp.zeros((1, 128), I32)
    for k in range(8):
        hit = lane == p * 8 + k
        end_l = jnp.where(hit, ends[k], end_l)
        start_l = jnp.where(hit, starts[k], start_l)
    gsrc[:, cols : cols + 128] = jnp.broadcast_to(end_l.astype(F32), (8, 128))
    gsrc[:, cols + 128 :] = jnp.broadcast_to(start_l.astype(F32), (8, 128))
    gbuf[p] = gsrc[...]

    drain(rtab.at[pl.ds(0, (np_ - 1) * ns)], ry_r)
    table = rtab[...].reshape(peers, rows)
    here = (table >> 7) == me
    before = mm(onehot(here), onehot(i0 < i1))
    slot1 = (table & 127).astype(F32) + 1.0
    place_u, spread_b = [], None
    wide = iota((peers, peers * 2 * blocks), 1)
    wide0 = iota((peers, peers * 2 * blocks), 0)
    shift_bits = {1: 1, 2: 2, 4: 3}[blocks]
    for k in range(2):
        zk = jnp.where(here & (before == float(k)), slot1, 0.0)
        col_k = jnp.sum(zk, axis=1, keepdims=True).astype(I32) - 1
        row_k = nt(jnp.ones((8, rows), BF), zk.astype(BF))[0:1].astype(I32) - 1
        place_u.append(onehot(col_k == iota((peers, rows), 1)))
        ut = onehot(iota((rows, peers), 0) == row_k)
        ek = onehot(((wide >> shift_bits) == wide0) & (((wide >> (shift_bits - 1)) & 1) == k))
        part = mm(ut, ek)
        spread_b = part if spread_b is None else spread_b + part
    narrow = iota((rows, peers * 2 * blocks), 1) & (blocks - 1)
    takes = [jnp.where(narrow == cb, spread_b, 0.0).astype(BF) for cb in range(blocks)]

    drain(rb.at[pl.ds(0, peers - 1)], d_r)
    arrived = rb[...].astype(F32).reshape(peers * 2 * blocks, 128).astype(BF)
    for cb in range(blocks):
        xbuf[h, :, cb * 128 : (cb + 1) * 128] = mm(takes[cb], arrived).astype(BF)

    right, left = lax.rem(h + 1, nh), lax.rem(h + nh - 1, nh)
    hr = rows // 2

    def xpart(b, half_):
        return xbuf.at[b, pl.ds(half_ * hr, hr)]

    xs = []
    for half_ in (0, 1):
        a = remote(xpart(h, half_), xpart(h, half_), x_s.at[half_], x_r.at[half_], head=right)
        a.start()
        b = remote(xpart(h, 1 - half_), xpart(h, 1 - half_), x_s.at[2 + half_], x_r.at[2 + half_], head=left)
        b.start()
        xs += [a, b]
    xs[0].wait_recv()
    a = remote(xpart(left, 0), xpart(left, 0), x_s.at[4], x_r.at[4], head=right)
    a.start()
    xs[1].wait_recv()
    b = remote(xpart(right, 1), xpart(right, 1), x_s.at[5], x_r.at[5], head=left)
    b.start()

    for k in range(1, np_):
        remote(gsrc, gbuf.at[p], g_s, g_r, pool=lax.rem(p + k, np_)).start()
    wo_fwd = []
    for k in range(1, nh):
        wo_sends[k - 1].wait_recv()
        src_h = lax.rem(h + nh - k, nh)
        cp = remote(wo_all.at[src_h, mine], wo_all.at[src_h, mine], wc_s.at[k], wc_r.at[k], seq=sib)
        cp.start()
        wo_fwd.append(cp)

    for c in (xs[2], xs[3], a, b):
        c.wait_recv()
    for c in xs + [a, b]:
        c.wait_send()

    feats = jnp.concatenate([xbuf[i] for i in range(nh)], axis=1).astype(F32)
    centred = feats - jnp.mean(feats, axis=1, keepdims=True)
    var = jnp.mean(centred * centred, axis=1, keepdims=True)
    normed = (centred * lax.rsqrt(var + EPS) * scale_ref[...] + shift_ref[...]).astype(BF)
    loads[1].wait()
    hw = wv.shape[2]
    heads = hw // HEAD_DIM
    head_same = onehot((iota((hw, hw), 0) >> 6) == (iota((hw, hw), 1) >> 6))

    def rms(v, gain):
        sq = v * v
        hi = sq.astype(BF)
        lo = (sq - hi.astype(F32)).astype(BF)
        mean_sq = (mm(hi, head_same) + mm(lo, head_same)) * (1.0 / HEAD_DIM)
        return (v * lax.rsqrt(mean_sq + EPS) * gain).astype(BF)

    gains = jnp.concatenate([gain_ref[...]] * heads, axis=1)
    kbuf[s] = rms(mm(normed, wv[1]), gains[1:2])
    vbuf[s] = jnp.transpose(mm(normed, wv[2])).astype(BF)

    def zat(d):
        return lax.rem(z + d + nz, nz)

    bufs = (kbuf, vbuf)
    live, sends, sibs = {}, [], {}

    def pass_on(src_z, j, d, hop):
        block = bufs[j].at[src_z * 2 + core]
        cp = remote(
            block, block, k_s.at[d, hop, j], k_r.at[d, hop, j], seq=zat(1 if d == 0 else -1) * 2 + core
        )
        cp.start()
        live[d, hop, j] = cp
        sends.append(cp)

    def to_sib(src_z, j, d, hop):
        block = bufs[j].at[src_z * 2 + core]
        cp = remote(block, block, c_s.at[d, hop, j], c_r.at[d, hop, j], seq=sib)
        cp.start()
        sibs[d, hop, j] = cp

    for j in (0, 1):
        pass_on(z, j, 0, 1)
        pass_on(z, j, 1, 1)
    for j in (0, 1):
        to_sib(z, j, 0, 0)

    query = rms(mm(normed, wv[0]), gains[0:1])
    q_t = jnp.transpose(query.astype(F32) * 0.125)
    feat_head = iota((hw, rows), 0) >> 6
    q_bd = jnp.concatenate([jnp.where(feat_head == i, q_t, 0.0) for i in range(heads)], axis=1).astype(BF)
    q_pos = s * rows + (iota((1, heads * rows), 1) & (rows - 1))
    q_start, q_end = jnp.zeros_like(q_pos), jnp.zeros_like(q_pos)
    for k in range(8):
        inside = (q_pos >= starts[k]) & (q_pos < ends[k])
        q_start = jnp.where(inside, starts[k], q_start)
        q_end = jnp.where(inside, ends[k], q_end)

    def attend(src_z, state):
        keys = kbuf[pl.ds(src_z * 2, 2)].reshape(2 * rows, hw)
        vals = jnp.concatenate([vbuf[src_z * 2], vbuf[src_z * 2 + 1]], axis=1)
        scores = mm(keys, q_bd)
        key_pos = src_z * (2 * rows) + iota(scores.shape, 0)
        scores = jnp.where((key_pos >= q_start) & (key_pos < q_end), scores, MASKED)
        top = jnp.max(scores, axis=0, keepdims=True)
        if state is not None:
            top = jnp.maximum(top, state[0])
        weights = jnp.exp(scores - top)
        summed = jnp.sum(weights, axis=0, keepdims=True)
        mixed = mm(vals, weights.astype(BF))
        if state is not None:
            decay = jnp.exp(state[0] - top)
            summed = summed + state[1] * decay
        for i in range(heads):
            f, q = slice(i * HEAD_DIM, (i + 1) * HEAD_DIM), slice(i * rows, (i + 1) * rows)
            if state is None:
                acc_ref[f, :] = mixed[f, q]
            else:
                acc_ref[f, :] = acc_ref[f, :] * decay[:, q] + mixed[f, q]
        return top, summed

    last = nz // 2
    ready = [(z, [(0, 0, 0), (0, 0, 1)])]
    state = None
    for hop in range(1, last + 1):
        coming = {}
        for j in (0, 1):
            for d in (0, 1):
                if (d, hop, j) not in live:
                    continue
                src_z = zat(-hop if d == 0 else hop)
                live[d, hop, j].wait_recv()
                if hop + 1 < last or (hop + 1 == last and d == j):
                    pass_on(src_z, j, d, hop + 1)
                to_sib(src_z, j, d, hop)
                coming.setdefault(d if hop < last else 0, (src_z, []))[1].append((d, hop, j))
        for src_z, keys_ in ready:
            for key in keys_:
                sibs[key].wait_recv()
            state = attend(src_z, state)
        ready = list(coming.values())
    for src_z, keys_ in ready:
        for key in keys_:
            sibs[key].wait_recv()
        state = attend(src_z, state)

    total_w = state[1]
    att = []
    for i in range(heads):
        f, q = slice(i * HEAD_DIM, (i + 1) * HEAD_DIM), slice(i * rows, (i + 1) * rows)
        att.append((acc_ref[f, :] / total_w[:, q]).astype(BF).astype(F32))
    att = jnp.concatenate(att, axis=0)
    ob = hw // 128
    att_st = jnp.concatenate(
        [jnp.transpose(att[cb * 128 : (cb + 1) * 128]) for cb in range(ob)], axis=0
    ).astype(BF)

    n2 = peers * 2 * ob
    ob_bits = {1: 0, 2: 1}[ob]
    tall, tall1 = iota((n2, peers), 0), iota((n2, peers), 1)
    picked = None
    for k in range(2):
        e2 = onehot(((tall >> (ob_bits + 1)) == tall1) & (((tall >> ob_bits) & 1) == k))
        part = mm(e2, place_u[k])
        picked = part if picked is None else picked + part
    lowbit = iota((n2, rows), 0) & (ob - 1)
    a3 = jnp.concatenate([jnp.where(lowbit == cb, picked, 0.0) for cb in range(ob)], axis=1).astype(BF)
    sb2[...] = mm(a3, att_st).reshape(peers, 2 * ob, 128).astype(BF)

    def send_back(k, carry):
        t = lax.rem(me + k, peers)
        remote(sb2.at[t], rb2.at[me], b_s, b_r, pool=t // ns, seq=lax.rem(t, ns)).start()
        return carry

    lax.fori_loop(1, peers, send_back, 0)
    rb2[me] = sb2[me]

    drain(gbuf.at[pl.ds(0, np_ - 1)], g_r)
    info = gbuf[...].reshape(np_ * 8, cols + 256)
    end_row = jnp.sum(gbuf[:, 0, cols : cols + 128], axis=0, keepdims=True)[:, : np_ * 8]
    start_row = jnp.sum(gbuf[:, 0, cols + 128 :], axis=0, keepdims=True)[:, : np_ * 8]
    group_bits = {2048: 11, 1024: 10, 512: 9}[ns * rows]
    base = r_col[:, : np_ * 8]
    pos = (base & (ns * rows - 1)).astype(F32)
    own = (base >> group_bits) == (iota((rows, np_ * 8), 1) >> 3)
    pick_g = onehot(own & (pos >= start_row) & (pos < end_row))
    gate = None
    for piece in split3(info[:, :cols]):
        part = mm(pick_g, piece.astype(BF))
        gate = part if gate is None else gate + part

    code2 = t_col * (2 * ob) + rank_col * ob
    drain(rb2.at[pl.ds(0, peers - 1)], b_r)
    back = rb2[...].astype(F32).reshape(n2, 128).astype(BF)
    wide2 = iota((rows, n2), 1)
    code2 = jnp.concatenate([code2] * (n2 // rows), axis=1)
    for cb in range(ob):
        og[h, :, cb * 128 : (cb + 1) * 128] = mm(onehot(wide2 == code2 + cb), back).astype(BF)
    os_ = []
    for k in (2, 1, 3) if nh == 4 else range(1, nh):
        cp = remote(og.at[h], og.at[h], o_s.at[k], o_r.at[k], head=lax.rem(h + k, nh))
        cp.start()
        os_.append(cp)
    for c in wo_fwd:
        c.wait_recv()
    for c in os_:
        c.wait_recv()
    projected = None
    for i in range(nh):
        part = mm(og[i], wo_all[i])
        projected = part if projected is None else projected + part
    out_ref[...] = (lat_ref[...].astype(F32) + gate * projected).astype(BF)

    for c in os_ + wo_fwd + wo_sends + sends + list(sibs.values()):
        c.wait_send()
    drain(rtab.at[pl.ds(0, ns - 1)], rz_s)
    drain(rtab.at[pl.ds(0, (np_ - 1) * ns)], ry_s)
    drain(rb.at[pl.ds(0, peers - 1)], d_s)
    drain(rb2.at[pl.ds(0, peers - 1)], b_s)
    drain(gbuf.at[pl.ds(0, np_ - 1)], g_s)


def local(np_, ns, nh, latents, route, seg_lengths, modulation, qkv_weight, qk_gain, out_weight):
    rows, cols = latents.shape
    peers = np_ * ns
    blocks = cols // 128
    hw = qkv_weight.shape[2]
    ob = hw // 128
    width = cols * nh
    vm = pl.BlockSpec(memory_space=pltpu.VMEM)
    hbm = pl.BlockSpec(memory_space=pl.ANY)
    D = pltpu.SemaphoreType.DMA
    V = pltpu.VMEM
    return pl.pallas_call(
        functools.partial(kernel, np_, ns, nh),
        out_shape=jax.ShapeDtypeStruct((rows, cols), BF),
        in_specs=[vm, vm, pl.BlockSpec(memory_space=pltpu.SMEM), vm, hbm, hbm, hbm],
        out_specs=vm,
        scratch_shapes=[
            V((peers, 2 * blocks, 128), BF), V((peers, 2 * blocks, 128), BF),
            V((peers, 2 * ob, 128), BF), V((peers, 2 * ob, 128), BF),
            V((peers, 1, 128), I32),
            V((nh, rows, cols), BF), V((nh, rows, hw), BF),
            V((8, 3 * width), F32), V((3, width, hw), BF), V((hw, width), BF), V((nh, hw, cols), BF),
            V((8, cols + 256), F32), V((np_, 8, cols + 256), F32),
            V((ns, rows, hw), BF), V((ns, hw, rows), BF),
            V((rows, width), F32), V((rows, width), F32), V((hw, rows), F32),
            pltpu.SemaphoreType.REGULAR, D((3,)),
            D, D, D, D, D, D, D((4,)), D((4,)), D((4,)), D((4,)), D((6,)), D((6,)), D, D,
            D((2, 5, 2)), D((2, 5, 2)), D((2, 5, 2)), D((2, 5, 2)), D, D, D((4,)), D((4,)),
        ],
        compiler_params=pltpu.CompilerParams(
            collective_id=0, has_side_effects=True, vmem_limit_bytes=56 << 20
        ),
    )(
        latents, route.reshape(1, rows), seg_lengths, qk_gain, modulation[0],
        qkv_weight.transpose(1, 0, 2), out_weight,
    )


def solution(mesh):
    np_, ns, nh = mesh.shape["pool"], mesh.shape["seq"], mesh.shape["head"]
    return jax.shard_map(
        functools.partial(local, np_, ns, nh),
        mesh=mesh,
        in_specs=(
            P(("pool", "seq"), "head"), P(("pool", "seq")), P("pool", None), P("pool", None, None),
            P(None, None, "head"), P(), P("head", None),
        ),
        out_specs=P(("pool", "seq"), "head"),
        check_vma=False,
    )
```

```python
import functools

import jax
import jax.numpy as jnp
from jax import lax
from jax.experimental import pallas as pl
from jax.experimental.pallas import tpu as pltpu
from jax.sharding import PartitionSpec as P

MESH = pl.DeviceIdType.MESH
HEAD_DIM = 64
EPS = 1e-06
MASKED = -1e30
BF = jnp.bfloat16
F32 = jnp.float32
I32 = jnp.int32


def mm(a, b):
    return lax.dot_general(a, b, (((1,), (0,)), ((), ())), preferred_element_type=F32)


def nt(a, b):
    return lax.dot_general(a, b, (((1,), (1,)), ((), ())), preferred_element_type=F32)


def iota(shape, dim):
    return lax.broadcasted_iota(I32, shape, dim)


def onehot(cond):
    return jnp.where(cond, 1.0, 0.0).astype(BF)


def split3(x):
    hi = x.astype(BF).astype(F32)
    mid = (x - hi).astype(BF).astype(F32)
    return hi, mid, x - hi - mid


def signal(sem, **ids):
    pl.semaphore_signal(sem, inc=1, device_id=ids, device_id_type=MESH)


def remote(src, dst, send, recv, **ids):
    return pltpu.make_async_remote_copy(
        src_ref=src, dst_ref=dst, send_sem=send, recv_sem=recv, device_id=ids, device_id_type=MESH
    )


def drain(ref, sem):
    pltpu.make_async_copy(ref, ref, sem).wait()


def kernel(
    np_, ns, nh,
    lat_hbm, route_hbm, len_hbm, gain_hbm, mod_hbm, w_hbm, wo_hbm,
    out_ref,
    lat_ref, route_ref, len_ref, gain_ref, sb, rb, sb2, rb2, rtab, xbuf, og, modv, wv, wov, wo_all, gsrc, gbuf,
    kv_send, kv_buf, q_send, q_buf, back_ref, scale_ref, shift_ref, acc_ref,
    stage_sem, load_sem,
    rz_s, rz_r, ry_s, ry_r, d_s, d_r, wo_s, wo_r, wc_s, wc_r, x_s, x_r, g_s, g_r,
    k_s, k_r, c_s, c_r, q_s, q_r, b_s, b_r, o_s, o_r,
):
    p, s, h = lax.axis_index("pool"), lax.axis_index("seq"), lax.axis_index("head")
    z, core = s // 2, lax.rem(s, 2)
    sib = s + 1 - 2 * core
    nz = ns // 2
    peers = np_ * ns
    me = p * ns + s
    rows, cols = lat_ref.shape
    width = cols * nh

    barrier = pltpu.get_barrier_semaphore()
    for k in range(1, ns):
        signal(barrier, seq=lax.rem(s + k, ns))
    for k in range(1, np_):
        signal(barrier, pool=lax.rem(p + k, np_))
    for k in range(1, nh):
        signal(barrier, head=lax.rem(h + k, nh))

    first = [
        pltpu.make_async_copy(route_hbm, route_ref, load_sem.at[3]),
        pltpu.make_async_copy(lat_hbm, lat_ref, load_sem.at[4]),
        pltpu.make_async_copy(len_hbm, len_ref, load_sem.at[5]),
        pltpu.make_async_copy(gain_hbm, gain_ref, load_sem.at[6]),
    ]
    for c in first:
        c.start()
    loads = [
        pltpu.make_async_copy(mod_hbm, modv, load_sem.at[0]),
        pltpu.make_async_copy(w_hbm, wv, load_sem.at[1]),
        pltpu.make_async_copy(wo_hbm, wov, load_sem.at[2]),
    ]
    for c in loads:
        c.start()

    first[0].wait()
    rt = route_ref[...]
    r_row = jnp.broadcast_to(rt, (rows, rows))
    r_col = jnp.transpose(r_row.astype(F32)).astype(I32)
    t_row, t_col = r_row >> 7, r_col >> 7
    i0, i1 = iota((rows, rows), 0), iota((rows, rows), 1)
    same_t = t_row == t_col
    rank_row = jnp.sum(jnp.where(same_t & (i0 < i1), 1.0, 0.0), axis=0, keepdims=True).astype(I32)
    rank_col = jnp.sum(jnp.where(same_t & (i1 < i0), 1.0, 0.0), axis=1, keepdims=True).astype(I32)
    first[1].wait()
    lat = lat_ref[...]
    blocks = cols // 128
    code = (rt >> 7) * (2 * blocks) + rank_row * blocks
    big = iota((peers * 2 * blocks, rows), 0)
    spread = jnp.concatenate([onehot(big == code + cb) for cb in range(blocks)], axis=1)
    stacked = jnp.concatenate([lat[:, cb * 128 : (cb + 1) * 128] for cb in range(blocks)], axis=0)
    sb[...] = mm(spread, stacked).reshape(peers, 2 * blocks, 128).astype(BF)
    rtab[me, 0] = rt[0]

    pl.semaphore_wait(barrier, ns + np_ + nh - 3)
    for k in range(1, np_):
        signal(stage_sem, pool=lax.rem(p + k, np_))

    for k in range(1, ns):
        remote(rtab.at[me], rtab.at[me], rz_s, rz_r, seq=lax.rem(s + k, ns)).start()

    def send_row(dp, ds):
        tp, ts = lax.rem(p + dp, np_), lax.rem(s + ds, ns)
        remote(sb.at[tp * ns + ts], rb.at[me], d_s, d_r, pool=tp, seq=ts).start()

    for k in range(1, ns):
        send_row(0, k)
    for k in range(1, np_):
        send_row(k, 0)
    rb[me] = sb[me]
    pl.semaphore_wait(stage_sem, np_ - 1)

    def send_rows(i, carry):
        a, b = i // (np_ - 1), lax.rem(i, np_ - 1)
        ds = lax.rem(ns // 2 + jnp.where(lax.rem(a, 2) == 0, a // 2, ns - (a + 1) // 2), ns)
        dp = lax.rem(np_ // 2 + jnp.where(lax.rem(b, 2) == 0, b // 2, np_ - (b + 1) // 2), np_)
        send_row(dp, ds)
        return carry

    lax.fori_loop(0, (ns - 1) * (np_ - 1), send_rows, 0)

    loads[2].wait()
    half = wov.shape[0] // 2
    mine = pl.ds(pl.multiple_of(core * half, half), half)
    other = pl.ds(pl.multiple_of((1 - core) * half, half), half)
    wo_sends = []
    for k in range(1, nh):
        t = lax.rem(h + k, nh)
        cp = remote(
            wov.at[mine, pl.ds(pl.multiple_of(t * cols, cols), cols)], wo_all.at[h, mine],
            wo_s.at[k], wo_r.at[k], head=t,
        )
        cp.start()
        wo_sends.append(cp)
    wo_all[h] = wov[:, pl.ds(pl.multiple_of(h * cols, cols), cols)]

    drain(rtab.at[pl.ds(0, ns - 1)], rz_r)
    own_line = rtab.at[pl.ds(pl.multiple_of(p * ns, ns), ns)]
    for k in range(1, np_):
        remote(own_line, own_line, ry_s, ry_r, pool=lax.rem(p + k, np_)).start()

    first[2].wait()
    first[3].wait()
    ends = []
    total = 0
    for k in range(8):
        total = total + len_ref[0, k]
        ends.append(total)
    starts = [0] + ends[:7]

    def lane_row(n, values, offset, period):
        lane = iota((1, n), 1)
        out = jnp.zeros((1, n), I32)
        for k in range(8):
            hit = (lane & (period - 1)) == offset + k
            out = jnp.where(hit, values[k], out)
        return out

    pos32 = s * rows + iota((rows, 32), 0)
    pick = onehot(
        (pos32 >= lane_row(32, starts, 0, 8)) & (pos32 < lane_row(32, ends, 0, 8)) & (iota((rows, 32), 1) < 24)
    )
    loads[0].wait()
    step = 1024
    for c in range(0, 2 * width, step):
        hi, mid, lo = split3(modv[:, c : c + step])
        table = jnp.concatenate([hi, mid, lo, jnp.zeros_like(lo)], axis=0).astype(BF)
        part = mm(pick, table)
        if c < width:
            shift_ref[:, c : c + step] = part
        else:
            scale_ref[:, c - width : c - width + step] = 1.0 + part
    gsrc[:, :cols] = modv[:, pl.ds(pl.multiple_of(2 * width + h * cols, cols), cols)]
    lane = iota((1, 128), 1)
    end_l, start_l = jnp.zeros((1, 128), I32), jnp.zeros((1, 128), I32)
    for k in range(8):
        hit = lane == p * 8 + k
        end_l = jnp.where(hit, ends[k], end_l)
        start_l = jnp.where(hit, starts[k], start_l)
    gsrc[:, cols : cols + 128] = jnp.broadcast_to(end_l.astype(F32), (8, 128))
    gsrc[:, cols + 128 :] = jnp.broadcast_to(start_l.astype(F32), (8, 128))
    gbuf[p] = gsrc[...]

    drain(rtab.at[pl.ds(0, (np_ - 1) * ns)], ry_r)
    table = rtab[...].reshape(peers, rows)
    here = (table >> 7) == me
    before = mm(onehot(here), onehot(i0 < i1))
    slot1 = (table & 127).astype(F32) + 1.0
    spread_b = None
    wide = iota((peers, peers * 2 * blocks), 1)
    wide0 = iota((peers, peers * 2 * blocks), 0)
    shift_bits = {1: 1, 2: 2, 4: 3}[blocks]
    for k in range(2):
        zk = jnp.where(here & (before == float(k)), slot1, 0.0)
        row_k = nt(jnp.ones((8, rows), BF), zk.astype(BF))[0:1].astype(I32) - 1
        ut = onehot(iota((rows, peers), 0) == row_k)
        ek = onehot(((wide >> shift_bits) == wide0) & (((wide >> (shift_bits - 1)) & 1) == k))
        part = mm(ut, ek)
        spread_b = part if spread_b is None else spread_b + part
    narrow = iota((rows, peers * 2 * blocks), 1) & (blocks - 1)
    takes = [jnp.where(narrow == cb, spread_b, 0.0).astype(BF) for cb in range(blocks)]

    drain(rb.at[pl.ds(0, peers - 1)], d_r)
    arrived = rb[...].astype(F32).reshape(peers * 2 * blocks, 128).astype(BF)
    for cb in range(blocks):
        xbuf[h, :, cb * 128 : (cb + 1) * 128] = mm(takes[cb], arrived).astype(BF)

    right, left = lax.rem(h + 1, nh), lax.rem(h + nh - 1, nh)
    hr = rows // 4

    def xsend(b, part, i, to):
        block = xbuf.at[b, pl.ds(part * hr, hr)]
        cp = remote(block, block, x_s.at[i], x_r.at[i], head=to)
        cp.start()
        return cp

    to_right = [xsend(h, part, i, right) for i, part in enumerate((0, 1, 2, 3))]
    to_left = [xsend(h, part, 4 + i, left) for i, part in enumerate((2, 3, 0, 1))]
    onward = []
    for i in range(2):
        to_right[i].wait_recv()
        onward.append(xsend(left, i, 8 + i, right))
        to_left[i].wait_recv()
        onward.append(xsend(right, 2 + i, 10 + i, left))

    for k in range(1, np_):
        remote(gsrc, gbuf.at[p], g_s, g_r, pool=lax.rem(p + k, np_)).start()
    wo_fwd = []
    for k in range(1, nh):
        wo_sends[k - 1].wait_recv()
        src_h = lax.rem(h + nh - k, nh)
        cp = remote(wo_all.at[src_h, mine], wo_all.at[src_h, mine], wc_s.at[k], wc_r.at[k], seq=sib)
        cp.start()
        wo_fwd.append(cp)

    for c in to_right[2:] + to_left[2:] + onward:
        c.wait_recv()
    for c in to_right + to_left + onward:
        c.wait_send()

    feats = jnp.concatenate([xbuf[i] for i in range(nh)], axis=1).astype(F32)
    centred = feats - jnp.mean(feats, axis=1, keepdims=True)
    var = jnp.mean(centred * centred, axis=1, keepdims=True)
    normed = (centred * lax.rsqrt(var + EPS) * scale_ref[...] + shift_ref[...]).astype(BF)
    loads[1].wait()
    hw = wv.shape[2]
    heads = hw // HEAD_DIM
    head_same = onehot((iota((hw, hw), 0) >> 6) == (iota((hw, hw), 1) >> 6))

    def rms(v, gain):
        sq = v * v
        hi = sq.astype(BF)
        lo = (sq - hi.astype(F32)).astype(BF)
        mean_sq = (mm(hi, head_same) + mm(lo, head_same)) * (1.0 / HEAD_DIM)
        return (v * lax.rsqrt(mean_sq + EPS) * gain).astype(BF)

    gains = jnp.concatenate([gain_ref[...]] * heads, axis=1)
    keys = rms(mm(normed, wv[1]), gains[1:2])
    vals = mm(normed, wv[2]).astype(BF)
    from_lane, to_lane = iota((hw, 2 * hw), 0), iota((hw, 2 * hw), 1)
    at_lane = (from_lane >> 6) * 128 + (from_lane & 63)
    kv = mm(keys, onehot(to_lane == at_lane)) + mm(vals, onehot(to_lane == at_lane + 64))
    for i in range(heads):
        kv_send[i] = kv[:, i * 128 : (i + 1) * 128].astype(BF)

    def zat(d):
        return lax.rem(z + d + nz, nz)

    my_head, my_quarter = z // 2, lax.rem(z, 2) * 2 + core
    near = []
    for d in range(1, nz // 2 + 1):
        near += [d, nz - d] if 2 * d < nz else [d]
    kv_live, sibs = {}, {}
    for d in reversed(near):
        to = zat(d)
        kv_live[d] = remote(kv_send.at[to // 2], kv_buf.at[s], k_s.at[d], k_r.at[d], seq=to * 2 + core)
        kv_live[d].start()

    def to_sib(d):
        block = kv_buf.at[zat(-d) * 2 + core]
        sibs[d] = remote(block, block, c_s.at[d], c_r.at[d], seq=sib)
        sibs[d].start()

    kv_buf[s] = kv_send[my_head]
    to_sib(0)

    query = rms(mm(normed, wv[0]), gains[0:1])
    q_send[...] = jnp.transpose(query.astype(F32) * 0.125).astype(BF).reshape(heads, HEAD_DIM, rows)
    quarter, part_of = s // 4, lax.rem(s, 4)

    def q_copy(i):
        to = i * 4 + quarter
        return to, remote(q_send.at[i], q_buf.at[part_of], q_s.at[i], q_r.at[part_of], seq=to)

    for i in range(heads):
        to, cp = q_copy(i)

        @pl.when(to != s)
        def _():
            cp.start()

        @pl.when(to == s)
        def _():
            q_buf[part_of] = q_send[i]

    n2 = peers * 4
    tall, tall1 = iota((n2, peers), 0), iota((n2, peers), 1)
    backs = [[], []]
    for t in range(4):
        here_t = (table >> 7) == p * ns + my_quarter * 4 + t
        before_t = mm(onehot(here_t), onehot(i0 < i1))
        e_t = onehot(tall == tall1 * 4 + t)
        for k in range(2):
            zk = jnp.where(here_t & (before_t == float(k)), slot1, 0.0)
            col_k = jnp.sum(zk, axis=1, keepdims=True).astype(I32) - 1
            backs[k].append(mm(e_t, onehot(col_k == iota((peers, rows), 1))).astype(BF))
    for k in range(2):
        for t in range(4):
            back_ref[k, :, t * rows : (t + 1) * rows] = backs[k][t]

    q_pos = my_quarter * (4 * rows) + iota((1, 4 * rows), 1)
    q_start, q_end = jnp.zeros_like(q_pos), jnp.zeros_like(q_pos)
    for k in range(8):
        inside = (q_pos >= starts[k]) & (q_pos < ends[k])
        q_start = jnp.where(inside, starts[k], q_start)
        q_end = jnp.where(inside, ends[k], q_end)

    for i in range(4):
        @pl.when(my_quarter * 4 + i != s)
        def _():
            remote(q_send.at[0], q_buf.at[i], q_s.at[0], q_r.at[i], seq=sib).wait_recv()

    q_pad = jnp.concatenate(
        [jnp.concatenate([q_buf[i] for i in range(4)], axis=1), jnp.zeros((HEAD_DIM, 4 * rows), BF)], axis=0
    )

    def attend(src_z, state):
        block = kv_buf[pl.ds(src_z * 2, 2)].reshape(2 * rows, 2 * HEAD_DIM)
        values_t = jnp.transpose(block.astype(F32))[HEAD_DIM:].astype(BF)
        scores = mm(block, q_pad)
        key_pos = src_z * (2 * rows) + iota(scores.shape, 0)
        scores = jnp.where((key_pos >= q_start) & (key_pos < q_end), scores, MASKED)
        top = jnp.max(scores, axis=0, keepdims=True)
        if state is not None:
            top = jnp.maximum(top, state[0])
        weights = jnp.exp(scores - top)
        summed = jnp.sum(weights, axis=0, keepdims=True)
        mixed = mm(values_t, weights.astype(BF))
        if state is None:
            acc_ref[...] = mixed
        else:
            decay = jnp.exp(state[0] - top)
            summed = summed + state[1] * decay
            acc_ref[...] = acc_ref[...] * decay + mixed
        return top, summed

    state = None
    ready = [0]
    for d in near:
        kv_live[d].wait_recv()
        to_sib(d)
        if len(ready) > 1 or d == near[0]:
            first = ready.pop(0)
            sibs[first].wait_recv()
            state = attend(zat(-first), state)
        ready.append(d)
    for d in ready:
        sibs[d].wait_recv()
        state = attend(zat(-d), state)

    att = (acc_ref[...] / state[1]).astype(BF).astype(F32)
    zeros = jnp.zeros_like(att)
    sent = mm(back_ref[0], jnp.transpose(jnp.concatenate([att, zeros], axis=0)).astype(BF))
    sent = sent + mm(back_ref[1], jnp.transpose(jnp.concatenate([zeros, att], axis=0)).astype(BF))
    sb2[...] = sent.reshape(peers, 4, 128).astype(BF)

    def send_back(k, carry):
        t = lax.rem(me + k, peers)
        remote(sb2.at[t], rb2.at[me], b_s, b_r, pool=t // ns, seq=lax.rem(t, ns)).start()
        return carry

    lax.fori_loop(1, peers, send_back, 0)
    rb2[me] = sb2[me]

    drain(gbuf.at[pl.ds(0, np_ - 1)], g_r)
    info = gbuf[...].reshape(np_ * 8, cols + 256)
    end_row = jnp.sum(gbuf[:, 0, cols : cols + 128], axis=0, keepdims=True)[:, : np_ * 8]
    start_row = jnp.sum(gbuf[:, 0, cols + 128 :], axis=0, keepdims=True)[:, : np_ * 8]
    group_bits = {2048: 11, 1024: 10, 512: 9}[ns * rows]
    base = r_col[:, : np_ * 8]
    pos = (base & (ns * rows - 1)).astype(F32)
    own = (base >> group_bits) == (iota((rows, np_ * 8), 1) >> 3)
    pick_g = onehot(own & (pos >= start_row) & (pos < end_row))
    gate = None
    for piece in split3(info[:, :cols]):
        part = mm(pick_g, piece.astype(BF))
        gate = part if gate is None else gate + part

    drain(rb2.at[pl.ds(0, peers - 1)], b_r)
    back = rb2[...].astype(F32).reshape(n2, 128).astype(BF)
    wide2 = iota((rows, n2), 1)
    code2 = (t_col >> 4) * 64 + (t_col & 15)
    code2 = jnp.concatenate([code2] * (n2 // rows), axis=1)
    low = iota((rows, 128), 1) < HEAD_DIM
    as_is = low == (rank_col == 0)
    for cb in range(heads // 2):
        first = mm(onehot(wide2 == code2 + 16 * (2 * cb)), back)
        second = mm(onehot(wide2 == code2 + 16 * (2 * cb + 1)), back)
        both = jnp.where(low, first, second)
        swapped = pltpu.roll(jnp.where(low, second, first), HEAD_DIM, 1)
        og[h, :, cb * 128 : (cb + 1) * 128] = jnp.where(as_is, both, swapped).astype(BF)
    os_ = []
    for k in (2, 1, 3) if nh == 4 else range(1, nh):
        cp = remote(og.at[h], og.at[h], o_s.at[k], o_r.at[k], head=lax.rem(h + k, nh))
        cp.start()
        os_.append(cp)
    for c in wo_fwd:
        c.wait_recv()
    for c in os_:
        c.wait_recv()
    projected = None
    for i in range(nh):
        part = mm(og[i], wo_all[i])
        projected = part if projected is None else projected + part
    out_ref[...] = gate * projected

    for c in os_ + wo_fwd + wo_sends + list(kv_live.values()) + list(sibs.values()):
        c.wait_send()
    for i in range(heads):
        to, cp = q_copy(i)

        @pl.when(to != s)
        def _():
            cp.wait_send()

    drain(rtab.at[pl.ds(0, ns - 1)], rz_s)
    drain(rtab.at[pl.ds(0, (np_ - 1) * ns)], ry_s)
    drain(rb.at[pl.ds(0, peers - 1)], d_s)
    drain(rb2.at[pl.ds(0, peers - 1)], b_s)
    drain(gbuf.at[pl.ds(0, np_ - 1)], g_s)


def local(np_, ns, nh, latents, route, seg_lengths, modulation, qkv_weight, qk_gain, out_weight):
    rows, cols = latents.shape
    peers = np_ * ns
    blocks = cols // 128
    hw = qkv_weight.shape[2]
    width = cols * nh
    vm = pl.BlockSpec(memory_space=pltpu.VMEM)
    hbm = pl.BlockSpec(memory_space=pl.ANY)
    D = pltpu.SemaphoreType.DMA
    V = pltpu.VMEM
    change = pl.pallas_call(
        functools.partial(kernel, np_, ns, nh),
        out_shape=jax.ShapeDtypeStruct((rows, cols), F32),
        in_specs=[hbm] * 7,
        out_specs=vm,
        scratch_shapes=[
            V((rows, cols), BF), V((1, rows), I32), pltpu.SMEM((1, 8), I32), V((2, HEAD_DIM), F32),
            V((peers, 2 * blocks, 128), BF), V((peers, 2 * blocks, 128), BF),
            V((peers, 4, 128), BF), V((peers, 4, 128), BF),
            V((peers, 1, 128), I32),
            V((nh, rows, cols), BF), V((nh, rows, hw), BF),
            V((8, 3 * width), F32), V((3, width, hw), BF), V((hw, width), BF), V((nh, hw, cols), BF),
            V((8, cols + 256), F32), V((np_, 8, cols + 256), F32),
            V((4, rows, 128), BF), V((ns, rows, 128), BF), V((4, HEAD_DIM, rows), BF), V((4, HEAD_DIM, rows), BF),
            V((2, peers * 4, 4 * rows), BF), V((rows, width), F32), V((rows, width), F32), V((HEAD_DIM, 4 * rows), F32),
            pltpu.SemaphoreType.REGULAR, D((7,)),
            D, D, D, D, D, D, D((4,)), D((4,)), D((4,)), D((4,)), D((12,)), D((12,)), D, D,
            D((8,)), D((8,)), D((8,)), D((8,)), D((4,)), D((4,)), D, D, D((4,)), D((4,)),
        ],
        compiler_params=pltpu.CompilerParams(
            collective_id=0, has_side_effects=True, vmem_limit_bytes=56 << 20
        ),
    )(
        latents, route.reshape(1, rows), seg_lengths, qk_gain, modulation[0],
        qkv_weight.transpose(1, 0, 2), out_weight,
    )
    return (latents.astype(F32) + change).astype(BF)


def solution(mesh):
    np_, ns, nh = mesh.shape["pool"], mesh.shape["seq"], mesh.shape["head"]
    return jax.shard_map(
        functools.partial(local, np_, ns, nh),
        mesh=mesh,
        in_specs=(
            P(("pool", "seq"), "head"), P(("pool", "seq")), P("pool", None), P("pool", None, None),
            P(None, None, "head"), P(), P("head", None),
        ),
        out_specs=P(("pool", "seq"), "head"),
        check_vma=False,
    )
```

```python
import functools

import jax
import jax.numpy as jnp
from jax import lax
from jax.experimental import pallas as pl
from jax.experimental.pallas import tpu as pltpu
from jax.sharding import PartitionSpec as P

MESH = pl.DeviceIdType.MESH
HEAD_DIM = 64
EPS = 1e-06
MASKED = -1e30
BF = jnp.bfloat16
F32 = jnp.float32
I32 = jnp.int32


def mm(a, b):
    return lax.dot_general(a, b, (((1,), (0,)), ((), ())), preferred_element_type=F32)


def nt(a, b):
    return lax.dot_general(a, b, (((1,), (1,)), ((), ())), preferred_element_type=F32)


def iota(shape, dim):
    return lax.broadcasted_iota(I32, shape, dim)


def onehot(cond):
    return jnp.where(cond, 1.0, 0.0).astype(BF)


def split3(x):
    hi = x.astype(BF).astype(F32)
    mid = (x - hi).astype(BF).astype(F32)
    return hi, mid, x - hi - mid


def signal(sem, **ids):
    pl.semaphore_signal(sem, inc=1, device_id=ids, device_id_type=MESH)


def remote(src, dst, send, recv, **ids):
    return pltpu.make_async_remote_copy(
        src_ref=src, dst_ref=dst, send_sem=send, recv_sem=recv, device_id=ids, device_id_type=MESH
    )


def drain(ref, sem):
    pltpu.make_async_copy(ref, ref, sem).wait()


def kernel(
    np_, ns, nh,
    lat_hbm, route_hbm, len_hbm, gain_hbm, mod_hbm, w_hbm, wo_hbm,
    out_ref,
    lat_ref, route_ref, len_ref, gain_ref, sb, rb, sb2, rb2, rtab, xbuf, og, modv, wv, wov, wo_all, gsrc, gbuf,
    kv_send, kv_buf, q_send, q_buf, back_ref, scale_ref, shift_ref, acc_ref,
    stage_sem, load_sem,
    rz_s, rz_r, ry_s, ry_r, d_s, d_r, wo_s, wo_r, wc_s, wc_r, x_s, x_r, g_s, g_r,
    k_s, k_r, c_s, c_r, q_s, q_r, b_s, b_r, o_s, o_r,
):
    p, s, h = lax.axis_index("pool"), lax.axis_index("seq"), lax.axis_index("head")
    z, core = s // 2, lax.rem(s, 2)
    sib = s + 1 - 2 * core
    nz = ns // 2
    peers = np_ * ns
    me = p * ns + s
    rows, cols = lat_ref.shape
    width = cols * nh

    barrier = pltpu.get_barrier_semaphore()
    for k in range(1, ns):
        signal(barrier, seq=lax.rem(s + k, ns))
    for k in range(1, np_):
        signal(barrier, pool=lax.rem(p + k, np_))
    for k in range(1, nh):
        signal(barrier, head=lax.rem(h + k, nh))

    first = [
        pltpu.make_async_copy(route_hbm, route_ref, load_sem.at[3]),
        pltpu.make_async_copy(lat_hbm, lat_ref, load_sem.at[4]),
        pltpu.make_async_copy(len_hbm, len_ref, load_sem.at[5]),
        pltpu.make_async_copy(gain_hbm, gain_ref, load_sem.at[6]),
    ]
    for c in first:
        c.start()
    loads = [
        pltpu.make_async_copy(mod_hbm, modv, load_sem.at[0]),
        pltpu.make_async_copy(w_hbm, wv, load_sem.at[1]),
        pltpu.make_async_copy(wo_hbm, wov, load_sem.at[2]),
    ]
    for c in loads:
        c.start()

    first[0].wait()
    rt = route_ref[...]
    r_row = jnp.broadcast_to(rt, (rows, rows))
    r_col = jnp.transpose(r_row.astype(F32)).astype(I32)
    t_row, t_col = r_row >> 7, r_col >> 7
    i0, i1 = iota((rows, rows), 0), iota((rows, rows), 1)
    same_t = t_row == t_col
    rank_row = jnp.sum(jnp.where(same_t & (i0 < i1), 1.0, 0.0), axis=0, keepdims=True).astype(I32)
    rank_col = jnp.sum(jnp.where(same_t & (i1 < i0), 1.0, 0.0), axis=1, keepdims=True).astype(I32)
    first[1].wait()
    lat = lat_ref[...]
    blocks = cols // 128
    code = (rt >> 7) * (2 * blocks) + rank_row * blocks
    big = iota((peers * 2 * blocks, rows), 0)
    spread = jnp.concatenate([onehot(big == code + cb) for cb in range(blocks)], axis=1)
    stacked = jnp.concatenate([lat[:, cb * 128 : (cb + 1) * 128] for cb in range(blocks)], axis=0)
    sb[...] = mm(spread, stacked).reshape(peers, 2 * blocks, 128).astype(BF)
    rtab[me, 0] = rt[0]

    pl.semaphore_wait(barrier, ns + np_ + nh - 3)
    for k in range(1, np_):
        signal(stage_sem, pool=lax.rem(p + k, np_))

    for k in range(1, ns):
        remote(rtab.at[me], rtab.at[me], rz_s, rz_r, seq=lax.rem(s + k, ns)).start()

    def send_row(dp, ds):
        tp, ts = lax.rem(p + dp, np_), lax.rem(s + ds, ns)
        remote(sb.at[tp * ns + ts], rb.at[me], d_s, d_r, pool=tp, seq=ts).start()

    for k in range(1, ns):
        send_row(0, k)
    for k in range(1, np_):
        send_row(k, 0)
    rb[me] = sb[me]
    pl.semaphore_wait(stage_sem, np_ - 1)

    def send_rows(i, carry):
        a, b = i // (np_ - 1), lax.rem(i, np_ - 1)
        ds = lax.rem(ns // 2 + jnp.where(lax.rem(a, 2) == 0, a // 2, ns - (a + 1) // 2), ns)
        dp = lax.rem(np_ // 2 + jnp.where(lax.rem(b, 2) == 0, b // 2, np_ - (b + 1) // 2), np_)
        send_row(dp, ds)
        return carry

    lax.fori_loop(0, (ns - 1) * (np_ - 1), send_rows, 0)

    loads[2].wait()
    half = wov.shape[0] // 2
    mine = pl.ds(pl.multiple_of(core * half, half), half)
    other = pl.ds(pl.multiple_of((1 - core) * half, half), half)
    wo_sends = []
    for k in range(1, nh):
        t = lax.rem(h + k, nh)
        cp = remote(
            wov.at[mine, pl.ds(pl.multiple_of(t * cols, cols), cols)], wo_all.at[h, mine],
            wo_s.at[k], wo_r.at[k], head=t,
        )
        cp.start()
        wo_sends.append(cp)
    wo_all[h] = wov[:, pl.ds(pl.multiple_of(h * cols, cols), cols)]

    drain(rtab.at[pl.ds(0, ns - 1)], rz_r)
    own_line = rtab.at[pl.ds(pl.multiple_of(p * ns, ns), ns)]
    for k in range(1, np_):
        remote(own_line, own_line, ry_s, ry_r, pool=lax.rem(p + k, np_)).start()

    first[2].wait()
    first[3].wait()
    ends = []
    total = 0
    for k in range(8):
        total = total + len_ref[0, k]
        ends.append(total)
    starts = [0] + ends[:7]

    def lane_row(n, values, offset, period):
        lane = iota((1, n), 1)
        out = jnp.zeros((1, n), I32)
        for k in range(8):
            hit = (lane & (period - 1)) == offset + k
            out = jnp.where(hit, values[k], out)
        return out

    pos32 = s * rows + iota((rows, 32), 0)
    pick = onehot(
        (pos32 >= lane_row(32, starts, 0, 8)) & (pos32 < lane_row(32, ends, 0, 8)) & (iota((rows, 32), 1) < 24)
    )
    loads[0].wait()
    step = 1024
    for c in range(0, 2 * width, step):
        hi, mid, lo = split3(modv[:, c : c + step])
        table = jnp.concatenate([hi, mid, lo, jnp.zeros_like(lo)], axis=0).astype(BF)
        part = mm(pick, table)
        if c < width:
            shift_ref[:, c : c + step] = part
        else:
            scale_ref[:, c - width : c - width + step] = 1.0 + part
    gsrc[:, :cols] = modv[:, pl.ds(pl.multiple_of(2 * width + h * cols, cols), cols)]
    lane = iota((1, 128), 1)
    end_l, start_l = jnp.zeros((1, 128), I32), jnp.zeros((1, 128), I32)
    for k in range(8):
        hit = lane == p * 8 + k
        end_l = jnp.where(hit, ends[k], end_l)
        start_l = jnp.where(hit, starts[k], start_l)
    gsrc[:, cols : cols + 128] = jnp.broadcast_to(end_l.astype(F32), (8, 128))
    gsrc[:, cols + 128 :] = jnp.broadcast_to(start_l.astype(F32), (8, 128))
    gbuf[p] = gsrc[...]

    drain(rtab.at[pl.ds(0, (np_ - 1) * ns)], ry_r)
    table = rtab[...].reshape(peers, rows)
    here = (table >> 7) == me
    before = mm(onehot(here), onehot(i0 < i1))
    slot1 = (table & 127).astype(F32) + 1.0
    spread_b = None
    wide = iota((peers, peers * 2 * blocks), 1)
    wide0 = iota((peers, peers * 2 * blocks), 0)
    shift_bits = {1: 1, 2: 2, 4: 3}[blocks]
    for k in range(2):
        zk = jnp.where(here & (before == float(k)), slot1, 0.0)
        row_k = nt(jnp.ones((8, rows), BF), zk.astype(BF))[0:1].astype(I32) - 1
        ut = onehot(iota((rows, peers), 0) == row_k)
        ek = onehot(((wide >> shift_bits) == wide0) & (((wide >> (shift_bits - 1)) & 1) == k))
        part = mm(ut, ek)
        spread_b = part if spread_b is None else spread_b + part
    narrow = iota((rows, peers * 2 * blocks), 1) & (blocks - 1)
    takes = [jnp.where(narrow == cb, spread_b, 0.0).astype(BF) for cb in range(blocks)]

    drain(rb.at[pl.ds(0, peers - 1)], d_r)
    arrived = rb[...].astype(F32).reshape(peers * 2 * blocks, 128).astype(BF)
    for cb in range(blocks):
        xbuf[h, :, cb * 128 : (cb + 1) * 128] = mm(takes[cb], arrived).astype(BF)

    right, left = lax.rem(h + 1, nh), lax.rem(h + nh - 1, nh)
    hr = rows // 4

    def xsend(b, part, i, to):
        block = xbuf.at[b, pl.ds(part * hr, hr)]
        cp = remote(block, block, x_s.at[i], x_r.at[i], head=to)
        cp.start()
        return cp

    to_right = [xsend(h, part, i, right) for i, part in enumerate((0, 1, 2, 3))]
    to_left = [xsend(h, part, 4 + i, left) for i, part in enumerate((2, 3, 0, 1))]
    onward = []
    for i in range(2):
        to_right[i].wait_recv()
        onward.append(xsend(left, i, 8 + i, right))
        to_left[i].wait_recv()
        onward.append(xsend(right, 2 + i, 10 + i, left))

    for k in range(1, np_):
        remote(gsrc, gbuf.at[p], g_s, g_r, pool=lax.rem(p + k, np_)).start()
    wo_fwd = []
    for k in range(1, nh):
        wo_sends[k - 1].wait_recv()
        src_h = lax.rem(h + nh - k, nh)
        cp = remote(wo_all.at[src_h, mine], wo_all.at[src_h, mine], wc_s.at[k], wc_r.at[k], seq=sib)
        cp.start()
        wo_fwd.append(cp)

    for c in to_right[2:] + to_left[2:] + onward:
        c.wait_recv()

    feats = jnp.concatenate([xbuf[i] for i in range(nh)], axis=1).astype(F32)
    centred = feats - jnp.mean(feats, axis=1, keepdims=True)
    var = jnp.mean(centred * centred, axis=1, keepdims=True)
    normed = (centred * lax.rsqrt(var + EPS) * scale_ref[...] + shift_ref[...]).astype(BF)
    loads[1].wait()
    hw = wv.shape[2]
    heads = hw // HEAD_DIM
    head_same = onehot((iota((hw, hw), 0) >> 6) == (iota((hw, hw), 1) >> 6))

    def rms(v, gain):
        sq = v * v
        hi = sq.astype(BF)
        lo = (sq - hi.astype(F32)).astype(BF)
        mean_sq = (mm(hi, head_same) + mm(lo, head_same)) * (1.0 / HEAD_DIM)
        return (v * lax.rsqrt(mean_sq + EPS) * gain).astype(BF)

    gains = jnp.concatenate([gain_ref[...]] * heads, axis=1)
    query = rms(mm(normed, wv[0]), gains[0:1])
    q_send[...] = jnp.transpose(query.astype(F32) * 0.125).astype(BF).reshape(heads, HEAD_DIM, rows)
    quarter, part_of = s // 4, lax.rem(s, 4)

    def q_copy(i):
        to = i * 4 + quarter
        return to, remote(q_send.at[i], q_buf.at[part_of], q_s.at[i], q_r.at[part_of], seq=to)

    for i in range(heads):
        to, cp = q_copy(i)

        @pl.when(to != s)
        def _():
            cp.start()

        @pl.when(to == s)
        def _():
            q_buf[part_of] = q_send[i]

    keys = rms(mm(normed, wv[1]), gains[1:2])
    vals = mm(normed, wv[2]).astype(BF)
    from_lane, to_lane = iota((hw, 2 * hw), 0), iota((hw, 2 * hw), 1)
    at_lane = (from_lane >> 6) * 128 + (from_lane & 63)
    kv = mm(keys, onehot(to_lane == at_lane)) + mm(vals, onehot(to_lane == at_lane + 64))
    for i in range(heads):
        kv_send[i] = kv[:, i * 128 : (i + 1) * 128].astype(BF)

    def zat(d):
        return lax.rem(z + d + nz, nz)

    my_head, my_quarter = z // 2, lax.rem(z, 2) * 2 + core
    near = []
    for d in range(1, nz // 2 + 1):
        near += [d, nz - d] if 2 * d < nz else [d]
    kv_live, sibs = {}, {}
    near = near[::-1]
    for d in near:
        to = zat(d)
        kv_live[d] = remote(kv_send.at[to // 2], kv_buf.at[s], k_s.at[d], k_r.at[d], seq=to * 2 + core)
        kv_live[d].start()

    def to_sib(d):
        block = kv_buf.at[zat(-d) * 2 + core]
        sibs[d] = remote(block, block, c_s.at[d], c_r.at[d], seq=sib)
        sibs[d].start()

    kv_buf[s] = kv_send[my_head]
    to_sib(0)

    n2 = peers * 4
    tall, tall1 = iota((n2, peers), 0), iota((n2, peers), 1)
    backs = [[], []]
    for t in range(4):
        here_t = (table >> 7) == p * ns + my_quarter * 4 + t
        before_t = mm(onehot(here_t), onehot(i0 < i1))
        e_t = onehot(tall == tall1 * 4 + t)
        for k in range(2):
            zk = jnp.where(here_t & (before_t == float(k)), slot1, 0.0)
            col_k = jnp.sum(zk, axis=1, keepdims=True).astype(I32) - 1
            backs[k].append(mm(e_t, onehot(col_k == iota((peers, rows), 1))).astype(BF))
    for k in range(2):
        for t in range(4):
            back_ref[k, :, t * rows : (t + 1) * rows] = backs[k][t]

    q_pos = my_quarter * (4 * rows) + iota((1, 4 * rows), 1)
    q_start, q_end = jnp.zeros_like(q_pos), jnp.zeros_like(q_pos)
    for k in range(8):
        inside = (q_pos >= starts[k]) & (q_pos < ends[k])
        q_start = jnp.where(inside, starts[k], q_start)
        q_end = jnp.where(inside, ends[k], q_end)

    for i in range(4):
        @pl.when(my_quarter * 4 + i != s)
        def _():
            remote(q_send.at[0], q_buf.at[i], q_s.at[0], q_r.at[i], seq=sib).wait_recv()

    q_pad = jnp.concatenate(
        [jnp.concatenate([q_buf[i] for i in range(4)], axis=1), jnp.zeros((HEAD_DIM, 4 * rows), BF)], axis=0
    )

    def attend(src_z, state):
        block = kv_buf[pl.ds(src_z * 2, 2)].reshape(2 * rows, 2 * HEAD_DIM)
        values_t = jnp.transpose(block.astype(F32))[HEAD_DIM:].astype(BF)
        scores = mm(block, q_pad)
        key_pos = src_z * (2 * rows) + iota(scores.shape, 0)
        scores = jnp.where((key_pos >= q_start) & (key_pos < q_end), scores, MASKED)
        top = jnp.max(scores, axis=0, keepdims=True)
        if state is not None:
            top = jnp.maximum(top, state[0])
        weights = jnp.exp(scores - top)
        summed = jnp.sum(weights, axis=0, keepdims=True)
        mixed = mm(values_t, weights.astype(BF))
        if state is None:
            acc_ref[...] = mixed
        else:
            decay = jnp.exp(state[0] - top)
            summed = summed + state[1] * decay
            acc_ref[...] = acc_ref[...] * decay + mixed
        return top, summed

    state = None
    ready = [0]
    for d in near:
        kv_live[d].wait_recv()
        to_sib(d)
        if len(ready) > 1 or d == near[0]:
            first = ready.pop(0)
            sibs[first].wait_recv()
            state = attend(zat(-first), state)
        ready.append(d)
    for d in ready:
        sibs[d].wait_recv()
        state = attend(zat(-d), state)

    att = (acc_ref[...] / state[1]).astype(BF).astype(F32)
    zeros = jnp.zeros_like(att)
    sent = mm(back_ref[0], jnp.transpose(jnp.concatenate([att, zeros], axis=0)).astype(BF))
    sent = sent + mm(back_ref[1], jnp.transpose(jnp.concatenate([zeros, att], axis=0)).astype(BF))
    sb2[...] = sent.reshape(peers, 4, 128).astype(BF)

    def send_back(k, carry):
        t = lax.rem(me + k, peers)
        remote(sb2.at[t], rb2.at[me], b_s, b_r, pool=t // ns, seq=lax.rem(t, ns)).start()
        return carry

    lax.fori_loop(1, peers, send_back, 0)
    rb2[me] = sb2[me]

    drain(gbuf.at[pl.ds(0, np_ - 1)], g_r)
    info = gbuf[...].reshape(np_ * 8, cols + 256)
    end_row = jnp.sum(gbuf[:, 0, cols : cols + 128], axis=0, keepdims=True)[:, : np_ * 8]
    start_row = jnp.sum(gbuf[:, 0, cols + 128 :], axis=0, keepdims=True)[:, : np_ * 8]
    group_bits = {2048: 11, 1024: 10, 512: 9}[ns * rows]
    base = r_col[:, : np_ * 8]
    pos = (base & (ns * rows - 1)).astype(F32)
    own = (base >> group_bits) == (iota((rows, np_ * 8), 1) >> 3)
    pick_g = onehot(own & (pos >= start_row) & (pos < end_row))
    gate = None
    for piece in split3(info[:, :cols]):
        part = mm(pick_g, piece.astype(BF))
        gate = part if gate is None else gate + part

    drain(rb2.at[pl.ds(0, peers - 1)], b_r)
    back = rb2[...].astype(F32).reshape(n2, 128).astype(BF)
    wide2 = iota((rows, n2), 1)
    code2 = (t_col >> 4) * 64 + (t_col & 15)
    code2 = jnp.concatenate([code2] * (n2 // rows), axis=1)
    low = iota((rows, 128), 1) < HEAD_DIM
    as_is = low == (rank_col == 0)
    for cb in range(heads // 2):
        first = mm(onehot(wide2 == code2 + 16 * (2 * cb)), back)
        second = mm(onehot(wide2 == code2 + 16 * (2 * cb + 1)), back)
        both = jnp.where(low, first, second)
        swapped = pltpu.roll(jnp.where(low, second, first), HEAD_DIM, 1)
        og[h, :, cb * 128 : (cb + 1) * 128] = jnp.where(as_is, both, swapped).astype(BF)
    from_head = {}
    for k in (2, 1, 3) if nh == 4 else range(1, nh):
        from_head[k] = remote(og.at[h], og.at[h], o_s.at[k], o_r.at[k], head=lax.rem(h + k, nh))
        from_head[k].start()
    for c in wo_fwd:
        c.wait_recv()
    projected = mm(og[h], wo_all[h])
    for k in (1, 3, 2) if nh == 4 else range(1, nh):
        source = lax.rem(h + nh - k, nh)
        from_head[k].wait_recv()
        projected = projected + mm(og[source], wo_all[source])
    out_ref[...] = (lat_ref[...].astype(F32) + gate * projected).astype(BF)

    for c in to_right + to_left + onward + list(from_head.values()) + wo_fwd + wo_sends + list(kv_live.values()) + list(sibs.values()):
        c.wait_send()
    for i in range(heads):
        to, cp = q_copy(i)

        @pl.when(to != s)
        def _():
            cp.wait_send()

    drain(rtab.at[pl.ds(0, ns - 1)], rz_s)
    drain(rtab.at[pl.ds(0, (np_ - 1) * ns)], ry_s)
    drain(rb.at[pl.ds(0, peers - 1)], d_s)
    drain(rb2.at[pl.ds(0, peers - 1)], b_s)
    drain(gbuf.at[pl.ds(0, np_ - 1)], g_s)


def local(np_, ns, nh, latents, route, seg_lengths, modulation, qkv_weight, qk_gain, out_weight):
    rows, cols = latents.shape
    peers = np_ * ns
    blocks = cols // 128
    hw = qkv_weight.shape[2]
    width = cols * nh
    vm = pl.BlockSpec(memory_space=pltpu.VMEM)
    hbm = pl.BlockSpec(memory_space=pl.ANY)
    D = pltpu.SemaphoreType.DMA
    V = pltpu.VMEM
    change = pl.pallas_call(
        functools.partial(kernel, np_, ns, nh),
        out_shape=pltpu.VMEM((rows, cols), BF),
        in_specs=[hbm] * 7,
        out_specs=vm,
        scratch_shapes=[
            V((rows, cols), BF), V((1, rows), I32), pltpu.SMEM((1, 8), I32), V((2, HEAD_DIM), F32),
            V((peers, 2 * blocks, 128), BF), V((peers, 2 * blocks, 128), BF),
            V((peers, 4, 128), BF), V((peers, 4, 128), BF),
            V((peers, 1, 128), I32),
            V((nh, rows, cols), BF), V((nh, rows, hw), BF),
            V((8, 3 * width), F32), V((3, width, hw), BF), V((hw, width), BF), V((nh, hw, cols), BF),
            V((8, cols + 256), F32), V((np_, 8, cols + 256), F32),
            V((4, rows, 128), BF), V((ns, rows, 128), BF), V((4, HEAD_DIM, rows), BF), V((4, HEAD_DIM, rows), BF),
            V((2, peers * 4, 4 * rows), BF), V((rows, width), F32), V((rows, width), F32), V((HEAD_DIM, 4 * rows), F32),
            pltpu.SemaphoreType.REGULAR, D((7,)),
            D, D, D, D, D, D, D((4,)), D((4,)), D((4,)), D((4,)), D((12,)), D((12,)), D, D,
            D((8,)), D((8,)), D((8,)), D((8,)), D((4,)), D((4,)), D, D, D((4,)), D((4,)),
        ],
        compiler_params=pltpu.CompilerParams(
            collective_id=0, has_side_effects=True, vmem_limit_bytes=56 << 20
        ),
    )(
        latents, route.reshape(1, rows), seg_lengths, qk_gain, modulation[0],
        qkv_weight.transpose(1, 0, 2), out_weight,
    )
    return change


def solution(mesh):
    np_, ns, nh = mesh.shape["pool"], mesh.shape["seq"], mesh.shape["head"]
    return jax.shard_map(
        functools.partial(local, np_, ns, nh),
        mesh=mesh,
        in_specs=(
            P(("pool", "seq"), "head"), P(("pool", "seq")), P("pool", None), P("pool", None, None),
            P(None, None, "head"), P(), P("head", None),
        ),
        out_specs=P(("pool", "seq"), "head"),
        check_vma=False,
    )
```

```python
import functools

import jax
import jax.numpy as jnp
from jax import lax
from jax.experimental import pallas as pl
from jax.experimental.pallas import tpu as pltpu
from jax.sharding import PartitionSpec as P

MESH = pl.DeviceIdType.MESH
HEAD_DIM = 64
EPS = 1e-06
MASKED = -1e30
BF = jnp.bfloat16
F32 = jnp.float32
I32 = jnp.int32


def mm(a, b):
    return lax.dot_general(a, b, (((1,), (0,)), ((), ())), preferred_element_type=F32)


def nt(a, b):
    return lax.dot_general(a, b, (((1,), (1,)), ((), ())), preferred_element_type=F32)


def iota(shape, dim):
    return lax.broadcasted_iota(I32, shape, dim)


def onehot(cond):
    return jnp.where(cond, 1.0, 0.0).astype(BF)


def split3(x):
    hi = x.astype(BF).astype(F32)
    mid = (x - hi).astype(BF).astype(F32)
    return hi, mid, x - hi - mid


def signal(sem, **ids):
    pl.semaphore_signal(sem, inc=1, device_id=ids, device_id_type=MESH)


def remote(src, dst, send, recv, **ids):
    return pltpu.make_async_remote_copy(
        src_ref=src, dst_ref=dst, send_sem=send, recv_sem=recv, device_id=ids, device_id_type=MESH
    )


def drain(ref, sem):
    pltpu.make_async_copy(ref, ref, sem).wait()


def kernel(
    np_, ns, nh,
    lat_hbm, route_hbm, len_hbm, gain_hbm, mod_hbm, w_hbm, wo_hbm,
    out_ref,
    lat_ref, route_ref, len_ref, gain_ref, sb, rb, sb2, rb2, rtab, xbuf, og, modv, wv, wov, wo_all, gsrc, gbuf,
    kv_send, kv_buf, q_send, q_buf, back_ref, scale_ref, shift_ref, acc_ref,
    stage_sem, load_sem,
    rz_s, rz_r, ry_s, ry_r, d_s, d_r, wo_s, wo_r, wc_s, wc_r, x_s, x_r, g_s, g_r,
    k_s, k_r, c_s, c_r, q_s, q_r, b_s, b_r, o_s, o_r,
):
    p, s, h = lax.axis_index("pool"), lax.axis_index("seq"), lax.axis_index("head")
    z, core = s // 2, lax.rem(s, 2)
    sib = s + 1 - 2 * core
    nz = ns // 2
    peers = np_ * ns
    me = p * ns + s
    rows, cols = lat_ref.shape
    width = cols * nh

    barrier = pltpu.get_barrier_semaphore()
    for k in range(1, ns):
        signal(barrier, seq=lax.rem(s + k, ns))
    for k in range(1, np_):
        signal(barrier, pool=lax.rem(p + k, np_))
    for k in range(1, nh):
        signal(barrier, head=lax.rem(h + k, nh))

    first = [
        pltpu.make_async_copy(route_hbm, route_ref, load_sem.at[3]),
        pltpu.make_async_copy(lat_hbm, lat_ref, load_sem.at[4]),
        pltpu.make_async_copy(len_hbm, len_ref, load_sem.at[5]),
        pltpu.make_async_copy(gain_hbm, gain_ref, load_sem.at[6]),
    ]
    for c in first:
        c.start()
    loads = [
        pltpu.make_async_copy(mod_hbm, modv, load_sem.at[0]),
        pltpu.make_async_copy(w_hbm, wv, load_sem.at[1]),
        pltpu.make_async_copy(wo_hbm, wov, load_sem.at[2]),
    ]
    for c in loads:
        c.start()

    first[0].wait()
    rt = route_ref[...]
    r_row = jnp.broadcast_to(rt, (rows, rows))
    r_col = jnp.transpose(r_row.astype(F32)).astype(I32)
    t_row, t_col = r_row >> 7, r_col >> 7
    i0, i1 = iota((rows, rows), 0), iota((rows, rows), 1)
    same_t = t_row == t_col
    rank_row = jnp.sum(jnp.where(same_t & (i0 < i1), 1.0, 0.0), axis=0, keepdims=True).astype(I32)
    rank_col = jnp.sum(jnp.where(same_t & (i1 < i0), 1.0, 0.0), axis=1, keepdims=True).astype(I32)
    first[1].wait()
    lat = lat_ref[...]
    blocks = cols // 128
    code = (rt >> 7) * (2 * blocks) + rank_row * blocks
    big = iota((peers * 2 * blocks, rows), 0)
    spread = jnp.concatenate([onehot(big == code + cb) for cb in range(blocks)], axis=1)
    stacked = jnp.concatenate([lat[:, cb * 128 : (cb + 1) * 128] for cb in range(blocks)], axis=0)
    sb[...] = mm(spread, stacked).reshape(peers, 2 * blocks, 128).astype(BF)
    rtab[me, 0] = rt[0]

    pl.semaphore_wait(barrier, ns + np_ + nh - 3)
    for k in range(1, np_):
        signal(stage_sem, pool=lax.rem(p + k, np_))

    for k in range(1, ns):
        remote(rtab.at[me], rtab.at[me], rz_s, rz_r, seq=lax.rem(s + k, ns)).start()

    def send_row(dp, ds):
        tp, ts = lax.rem(p + dp, np_), lax.rem(s + ds, ns)
        remote(sb.at[tp * ns + ts], rb.at[me], d_s, d_r, pool=tp, seq=ts).start()

    for k in range(1, ns):
        send_row(0, k)
    for k in range(1, np_):
        send_row(k, 0)
    rb[me] = sb[me]
    pl.semaphore_wait(stage_sem, np_ - 1)

    def send_rows(i, carry):
        a, b = i // (np_ - 1), lax.rem(i, np_ - 1)
        ds = lax.rem(ns // 2 + jnp.where(lax.rem(a, 2) == 0, a // 2, ns - (a + 1) // 2), ns)
        dp = lax.rem(np_ // 2 + jnp.where(lax.rem(b, 2) == 0, b // 2, np_ - (b + 1) // 2), np_)
        send_row(dp, ds)
        return carry

    lax.fori_loop(0, (ns - 1) * (np_ - 1), send_rows, 0)

    drain(rtab.at[pl.ds(0, ns - 1)], rz_r)
    own_line = rtab.at[pl.ds(pl.multiple_of(p * ns, ns), ns)]
    for k in range(1, np_):
        remote(own_line, own_line, ry_s, ry_r, pool=lax.rem(p + k, np_)).start()

    loads[2].wait()
    half = wov.shape[0] // 2
    mine = pl.ds(pl.multiple_of(core * half, half), half)
    other = pl.ds(pl.multiple_of((1 - core) * half, half), half)
    wo_sends = []
    for k in range(1, nh):
        t = lax.rem(h + k, nh)
        cp = remote(
            wov.at[mine, pl.ds(pl.multiple_of(t * cols, cols), cols)], wo_all.at[h, mine],
            wo_s.at[k], wo_r.at[k], head=t,
        )
        cp.start()
        wo_sends.append(cp)
    wo_all[h] = wov[:, pl.ds(pl.multiple_of(h * cols, cols), cols)]

    first[2].wait()
    first[3].wait()
    ends = []
    total = 0
    for k in range(8):
        total = total + len_ref[0, k]
        ends.append(total)
    starts = [0] + ends[:7]

    def lane_row(n, values, offset, period):
        lane = iota((1, n), 1)
        out = jnp.zeros((1, n), I32)
        for k in range(8):
            hit = (lane & (period - 1)) == offset + k
            out = jnp.where(hit, values[k], out)
        return out

    pos32 = s * rows + iota((rows, 32), 0)
    pick = onehot(
        (pos32 >= lane_row(32, starts, 0, 8)) & (pos32 < lane_row(32, ends, 0, 8)) & (iota((rows, 32), 1) < 24)
    )
    loads[0].wait()
    step = 1024
    for c in range(0, 2 * width, step):
        hi, mid, lo = split3(modv[:, c : c + step])
        table = jnp.concatenate([hi, mid, lo, jnp.zeros_like(lo)], axis=0).astype(BF)
        part = mm(pick, table)
        if c < width:
            shift_ref[:, c : c + step] = part
        else:
            scale_ref[:, c - width : c - width + step] = 1.0 + part
    gsrc[:, :cols] = modv[:, pl.ds(pl.multiple_of(2 * width + h * cols, cols), cols)]
    lane = iota((1, 128), 1)
    end_l, start_l = jnp.zeros((1, 128), I32), jnp.zeros((1, 128), I32)
    for k in range(8):
        hit = lane == p * 8 + k
        end_l = jnp.where(hit, ends[k], end_l)
        start_l = jnp.where(hit, starts[k], start_l)
    gsrc[:, cols : cols + 128] = jnp.broadcast_to(end_l.astype(F32), (8, 128))
    gsrc[:, cols + 128 :] = jnp.broadcast_to(start_l.astype(F32), (8, 128))
    gbuf[p] = gsrc[...]

    drain(rtab.at[pl.ds(0, (np_ - 1) * ns)], ry_r)
    table = rtab[...].reshape(peers, rows)
    here = (table >> 7) == me
    before = mm(onehot(here), onehot(i0 < i1))
    slot1 = (table & 127).astype(F32) + 1.0
    spread_b = None
    wide = iota((peers, peers * 2 * blocks), 1)
    wide0 = iota((peers, peers * 2 * blocks), 0)
    shift_bits = {1: 1, 2: 2, 4: 3}[blocks]
    for k in range(2):
        zk = jnp.where(here & (before == float(k)), slot1, 0.0)
        row_k = nt(jnp.ones((8, rows), BF), zk.astype(BF))[0:1].astype(I32) - 1
        ut = onehot(iota((rows, peers), 0) == row_k)
        ek = onehot(((wide >> shift_bits) == wide0) & (((wide >> (shift_bits - 1)) & 1) == k))
        part = mm(ut, ek)
        spread_b = part if spread_b is None else spread_b + part
    narrow = iota((rows, peers * 2 * blocks), 1) & (blocks - 1)
    takes = [jnp.where(narrow == cb, spread_b, 0.0).astype(BF) for cb in range(blocks)]

    drain(rb.at[pl.ds(0, peers - 1)], d_r)
    arrived = rb[...].astype(F32).reshape(peers * 2 * blocks, 128).astype(BF)
    for cb in range(blocks):
        xbuf[h, :, cb * 128 : (cb + 1) * 128] = mm(takes[cb], arrived).astype(BF)

    right, left = lax.rem(h + 1, nh), lax.rem(h + nh - 1, nh)
    hr = rows // 4

    def xsend(b, part, i, to):
        block = xbuf.at[b, pl.ds(part * hr, hr)]
        cp = remote(block, block, x_s.at[i], x_r.at[i], head=to)
        cp.start()
        return cp

    to_right = [xsend(h, part, i, right) for i, part in enumerate((0, 1, 2, 3))]
    to_left = [xsend(h, part, 4 + i, left) for i, part in enumerate((2, 3, 0, 1))]
    onward = []
    for i in range(2):
        to_right[i].wait_recv()
        onward.append(xsend(left, i, 8 + i, right))
        to_left[i].wait_recv()
        onward.append(xsend(right, 2 + i, 10 + i, left))

    for k in range(1, np_):
        remote(gsrc, gbuf.at[p], g_s, g_r, pool=lax.rem(p + k, np_)).start()
    wo_fwd = []
    for k in range(1, nh):
        wo_sends[k - 1].wait_recv()
        src_h = lax.rem(h + nh - k, nh)
        cp = remote(wo_all.at[src_h, mine], wo_all.at[src_h, mine], wc_s.at[k], wc_r.at[k], seq=sib)
        cp.start()
        wo_fwd.append(cp)

    for c in to_right[2:] + to_left[2:] + onward:
        c.wait_recv()

    feats = jnp.concatenate([xbuf[i] for i in range(nh)], axis=1).astype(F32)
    centred = feats - jnp.mean(feats, axis=1, keepdims=True)
    var = jnp.mean(centred * centred, axis=1, keepdims=True)
    normed = (centred * lax.rsqrt(var + EPS) * scale_ref[...] + shift_ref[...]).astype(BF)
    loads[1].wait()
    hw = wv.shape[2]
    heads = hw // HEAD_DIM
    head_same = onehot((iota((hw, hw), 0) >> 6) == (iota((hw, hw), 1) >> 6))

    def rms(v, gain):
        sq = v * v
        hi = sq.astype(BF)
        lo = (sq - hi.astype(F32)).astype(BF)
        mean_sq = (mm(hi, head_same) + mm(lo, head_same)) * (1.0 / HEAD_DIM)
        return (v * lax.rsqrt(mean_sq + EPS) * gain).astype(BF)

    gains = jnp.concatenate([gain_ref[...]] * heads, axis=1)
    query = rms(mm(normed, wv[0]), gains[0:1])
    q_send[...] = jnp.transpose(query.astype(F32) * 0.125).astype(BF).reshape(heads, HEAD_DIM, rows)
    quarter, part_of = s // 4, lax.rem(s, 4)

    def q_copy(i):
        to = i * 4 + quarter
        return to, remote(q_send.at[i], q_buf.at[part_of], q_s.at[i], q_r.at[part_of], seq=to)

    for i in range(heads):
        to, cp = q_copy(i)

        @pl.when(to != s)
        def _():
            cp.start()

        @pl.when(to == s)
        def _():
            q_buf[part_of] = q_send[i]

    keys = rms(mm(normed, wv[1]), gains[1:2])
    vals = mm(normed, wv[2]).astype(BF)
    from_lane, to_lane = iota((hw, 2 * hw), 0), iota((hw, 2 * hw), 1)
    at_lane = (from_lane >> 6) * 128 + (from_lane & 63)
    kv = mm(keys, onehot(to_lane == at_lane)) + mm(vals, onehot(to_lane == at_lane + 64))
    for i in range(heads):
        kv_send[i] = kv[:, i * 128 : (i + 1) * 128].astype(BF)

    def zat(d):
        return lax.rem(z + d + nz, nz)

    my_head, my_quarter = z // 2, lax.rem(z, 2) * 2 + core
    near = []
    for d in range(1, nz // 2 + 1):
        near += [d, nz - d] if 2 * d < nz else [d]
    kv_live, sibs = {}, {}
    near = near[::-1]
    for d in near:
        to = zat(d)
        kv_live[d] = remote(kv_send.at[to // 2], kv_buf.at[s], k_s.at[d], k_r.at[d], seq=to * 2 + core)
        kv_live[d].start()

    def to_sib(d):
        block = kv_buf.at[zat(-d) * 2 + core]
        sibs[d] = remote(block, block, c_s.at[d], c_r.at[d], seq=sib)
        sibs[d].start()

    kv_buf[s] = kv_send[my_head]
    to_sib(0)

    n2 = peers * 4
    tall, tall1 = iota((n2, peers), 0), iota((n2, peers), 1)
    backs = [[], []]
    for t in range(4):
        here_t = (table >> 7) == p * ns + my_quarter * 4 + t
        before_t = mm(onehot(here_t), onehot(i0 < i1))
        e_t = onehot(tall == tall1 * 4 + t)
        for k in range(2):
            zk = jnp.where(here_t & (before_t == float(k)), slot1, 0.0)
            col_k = jnp.sum(zk, axis=1, keepdims=True).astype(I32) - 1
            backs[k].append(mm(e_t, onehot(col_k == iota((peers, rows), 1))).astype(BF))
    for k in range(2):
        for t in range(4):
            back_ref[k, :, t * rows : (t + 1) * rows] = backs[k][t]

    q_pos = my_quarter * (4 * rows) + iota((1, 4 * rows), 1)
    q_start, q_end = jnp.zeros_like(q_pos), jnp.zeros_like(q_pos)
    for k in range(8):
        inside = (q_pos >= starts[k]) & (q_pos < ends[k])
        q_start = jnp.where(inside, starts[k], q_start)
        q_end = jnp.where(inside, ends[k], q_end)

    for i in range(4):
        @pl.when(my_quarter * 4 + i != s)
        def _():
            remote(q_send.at[0], q_buf.at[i], q_s.at[0], q_r.at[i], seq=sib).wait_recv()

    q_pad = jnp.concatenate(
        [jnp.concatenate([q_buf[i] for i in range(4)], axis=1), jnp.zeros((HEAD_DIM, 4 * rows), BF)], axis=0
    )

    def attend(src_z, state):
        block = kv_buf[pl.ds(src_z * 2, 2)].reshape(2 * rows, 2 * HEAD_DIM)
        values_t = jnp.transpose(block.astype(F32))[HEAD_DIM:].astype(BF)
        scores = mm(block, q_pad)
        key_pos = src_z * (2 * rows) + iota(scores.shape, 0)
        scores = jnp.where((key_pos >= q_start) & (key_pos < q_end), scores, MASKED)
        top = jnp.max(scores, axis=0, keepdims=True)
        if state is not None:
            top = jnp.maximum(top, state[0])
        weights = jnp.exp(scores - top)
        summed = jnp.sum(weights, axis=0, keepdims=True)
        mixed = mm(values_t, weights.astype(BF))
        if state is None:
            acc_ref[...] = mixed
        else:
            decay = jnp.exp(state[0] - top)
            summed = summed + state[1] * decay
            acc_ref[...] = acc_ref[...] * decay + mixed
        return top, summed

    state = None
    ready = [0]
    for d in near:
        kv_live[d].wait_recv()
        to_sib(d)
        if len(ready) > 1 or d == near[0]:
            first = ready.pop(0)
            sibs[first].wait_recv()
            state = attend(zat(-first), state)
        ready.append(d)
    for d in ready:
        sibs[d].wait_recv()
        state = attend(zat(-d), state)

    att = (acc_ref[...] / state[1]).astype(BF).astype(F32)
    zeros = jnp.zeros_like(att)
    sent = mm(back_ref[0], jnp.transpose(jnp.concatenate([att, zeros], axis=0)).astype(BF))
    sent = sent + mm(back_ref[1], jnp.transpose(jnp.concatenate([zeros, att], axis=0)).astype(BF))
    sb2[...] = sent.reshape(peers, 4, 128).astype(BF)

    def send_back(k, carry):
        t = lax.rem(me + k, peers)
        remote(sb2.at[t], rb2.at[me], b_s, b_r, pool=t // ns, seq=lax.rem(t, ns)).start()
        return carry

    lax.fori_loop(1, peers, send_back, 0)
    rb2[me] = sb2[me]

    drain(gbuf.at[pl.ds(0, np_ - 1)], g_r)
    info = gbuf[...].reshape(np_ * 8, cols + 256)
    end_row = jnp.sum(gbuf[:, 0, cols : cols + 128], axis=0, keepdims=True)[:, : np_ * 8]
    start_row = jnp.sum(gbuf[:, 0, cols + 128 :], axis=0, keepdims=True)[:, : np_ * 8]
    group_bits = {2048: 11, 1024: 10, 512: 9}[ns * rows]
    base = r_col[:, : np_ * 8]
    pos = (base & (ns * rows - 1)).astype(F32)
    own = (base >> group_bits) == (iota((rows, np_ * 8), 1) >> 3)
    pick_g = onehot(own & (pos >= start_row) & (pos < end_row))
    gate = None
    for piece in split3(info[:, :cols]):
        part = mm(pick_g, piece.astype(BF))
        gate = part if gate is None else gate + part

    drain(rb2.at[pl.ds(0, peers - 1)], b_r)
    back = rb2[...].astype(F32).reshape(n2, 128).astype(BF)
    wide2 = iota((rows, n2), 1)
    code2 = (t_col >> 4) * 64 + (t_col & 15)
    code2 = jnp.concatenate([code2] * (n2 // rows), axis=1)
    low = iota((rows, 128), 1) < HEAD_DIM
    as_is = low == (rank_col == 0)
    for cb in range(heads // 2):
        first = mm(onehot(wide2 == code2 + 16 * (2 * cb)), back)
        second = mm(onehot(wide2 == code2 + 16 * (2 * cb + 1)), back)
        both = jnp.where(low, first, second)
        swapped = pltpu.roll(jnp.where(low, second, first), HEAD_DIM, 1)
        og[h, :, cb * 128 : (cb + 1) * 128] = jnp.where(as_is, both, swapped).astype(BF)
    from_head = {}
    for k in (2, 1, 3) if nh == 4 else range(1, nh):
        from_head[k] = remote(og.at[h], og.at[h], o_s.at[k], o_r.at[k], head=lax.rem(h + k, nh))
        from_head[k].start()
    for c in wo_fwd:
        c.wait_recv()
    projected = mm(og[h], wo_all[h])
    for k in (1, 3, 2) if nh == 4 else range(1, nh):
        source = lax.rem(h + nh - k, nh)
        from_head[k].wait_recv()
        projected = projected + mm(og[source], wo_all[source])
    out_ref[...] = (lat_ref[...].astype(F32) + gate * projected).astype(BF)

    for c in to_right + to_left + onward + list(from_head.values()) + wo_fwd + wo_sends + list(kv_live.values()) + list(sibs.values()):
        c.wait_send()
    for i in range(heads):
        to, cp = q_copy(i)

        @pl.when(to != s)
        def _():
            cp.wait_send()

    drain(rtab.at[pl.ds(0, ns - 1)], rz_s)
    drain(rtab.at[pl.ds(0, (np_ - 1) * ns)], ry_s)
    drain(rb.at[pl.ds(0, peers - 1)], d_s)
    drain(rb2.at[pl.ds(0, peers - 1)], b_s)
    drain(gbuf.at[pl.ds(0, np_ - 1)], g_s)


def local(np_, ns, nh, latents, route, seg_lengths, modulation, qkv_weight, qk_gain, out_weight):
    rows, cols = latents.shape
    peers = np_ * ns
    blocks = cols // 128
    hw = qkv_weight.shape[2]
    width = cols * nh
    vm = pl.BlockSpec(memory_space=pltpu.VMEM)
    hbm = pl.BlockSpec(memory_space=pl.ANY)
    D = pltpu.SemaphoreType.DMA
    V = pltpu.VMEM
    change = pl.pallas_call(
        functools.partial(kernel, np_, ns, nh),
        out_shape=pltpu.VMEM((rows, cols), BF),
        in_specs=[hbm] * 7,
        out_specs=vm,
        scratch_shapes=[
            V((rows, cols), BF), V((1, rows), I32), pltpu.SMEM((1, 8), I32), V((2, HEAD_DIM), F32),
            V((peers, 2 * blocks, 128), BF), V((peers, 2 * blocks, 128), BF),
            V((peers, 4, 128), BF), V((peers, 4, 128), BF),
            V((peers, 1, 128), I32),
            V((nh, rows, cols), BF), V((nh, rows, hw), BF),
            V((8, 3 * width), F32), V((3, width, hw), BF), V((hw, width), BF), V((nh, hw, cols), BF),
            V((8, cols + 256), F32), V((np_, 8, cols + 256), F32),
            V((4, rows, 128), BF), V((ns, rows, 128), BF), V((4, HEAD_DIM, rows), BF), V((4, HEAD_DIM, rows), BF),
            V((2, peers * 4, 4 * rows), BF), V((rows, width), F32), V((rows, width), F32), V((HEAD_DIM, 4 * rows), F32),
            pltpu.SemaphoreType.REGULAR, D((7,)),
            D, D, D, D, D, D, D((4,)), D((4,)), D((4,)), D((4,)), D((12,)), D((12,)), D, D,
            D((8,)), D((8,)), D((8,)), D((8,)), D((4,)), D((4,)), D, D, D((4,)), D((4,)),
        ],
        compiler_params=pltpu.CompilerParams(
            collective_id=0, has_side_effects=True, vmem_limit_bytes=56 << 20
        ),
    )(
        latents, route.reshape(1, rows), seg_lengths, qk_gain, modulation[0],
        qkv_weight.transpose(1, 0, 2), out_weight,
    )
    return change


def solution(mesh):
    np_, ns, nh = mesh.shape["pool"], mesh.shape["seq"], mesh.shape["head"]
    return jax.shard_map(
        functools.partial(local, np_, ns, nh),
        mesh=mesh,
        in_specs=(
            P(("pool", "seq"), "head"), P(("pool", "seq")), P("pool", None), P("pool", None, None),
            P(None, None, "head"), P(), P("head", None),
        ),
        out_specs=P(("pool", "seq"), "head"),
        check_vma=False,
    )
```
